256 devices in a mesh: chain: 32 (over z, x_hi, core), tok: 8 (over x_lo, y).
Axes of the slice: x: 4 (x_hi: 2, x_lo: 2; x = x_hi * 2 + x_lo), y: 4, z: 8, core: 2. Of those that a mesh axis runs over, the one named last changes fastest.
Arguments:
- queries: bfloat16 [524288, 128], P(('chain', 'tok')), may hold values from -6 to 6
- keys: bfloat16 [524288, 128], P(('chain', 'tok')), may hold values from -6 to 6
- values: bfloat16 [524288, 128], P(('chain', 'tok')), may hold values from -6 to 6
Outputs:
- attended: bfloat16 [524288, 128], P(('chain', 'tok'))
The draws below stay inside these ranges and needn't reach their ends.
All inputs are finite; a program needn't handle non-finite values.
Results may differ from the reference program's by a relative error of at most 0.0058.
Values may be sent and summed in bfloat16 or wider, within the bound.
No kernel may reach another device: no remote copies, remote signals or barrier semaphores. Data moves between devices by JAX's collectives and lax.ppermute only.
A program may use at most 64 MiB of HBM per device.

```python
import math
import jax
import jax.numpy as jnp
import numpy as np
from jax import lax

HD = 64
HEADS = 2
F = 2080
GROUP = 16384
TOKENS = 524288
N_CHAIN = 32


def levels(key, shape, pieces, low, largest):
    factor_of, own = 1.0, jax.random.fold_in(key, 6)
    for dim, parts in pieces:
        draws = jnp.exp(jax.random.uniform(jax.random.fold_in(own, dim), (parts,), jnp.float32, low / len(pieces), largest / len(pieces)))
        factor_of = factor_of * jnp.repeat(draws, shape[dim] // parts).reshape([-1 if axis == dim else 1 for axis in range(len(shape))])
    return factor_of


def normal_values(own_key, dims, scale, reach, pieces=(), held_as=jnp.bfloat16):
    array = scale * jax.random.normal(own_key, dims, jnp.float32)
    if pieces:
        array = array * levels(own_key, dims, pieces, -0.22, 0.18)
    return jnp.clip(array, -reach, reach).astype(held_as)


def setup_inputs(seed: int = 0) -> dict:
    streams_of = jax.random.split(jax.random.key(seed), 4)
    return {
        "queries": normal_values(streams_of[0], (TOKENS, HEADS * HD), 1.0, 6.0, ((0, 256),)),
        "keys": normal_values(streams_of[1], (TOKENS, HEADS * HD), 1.0, 6.0, ((0, 256),)),
        "values": normal_values(streams_of[2], (TOKENS, HEADS * HD), 1.0, 6.0, ((0, 256),)),
    }


def tables(width):
    first, second = np.triu_indices(width)
    places = np.arange(width)[:, None]
    first_pick = (places == first[None, :]).astype(np.float32)
    second_pick = (places == second[None, :]).astype(np.float32)
    scaling = np.where(first < second, math.sqrt(2.0), 1.0).astype(np.float32)
    return (jnp.asarray(first_pick), jnp.asarray(second_pick), jnp.asarray(scaling))

def expand(vectors, first_pick, second_pick, scaling):
    wide = vectors.astype(jnp.float32)
    left = jnp.dot(wide, first_pick, precision=lax.Precision.HIGHEST)
    right = jnp.dot(wide, second_pick, precision=lax.Precision.HIGHEST)
    rounded = (left * right * scaling[None, :]).astype(jnp.bfloat16)
    return lax.optimization_barrier(rounded).astype(jnp.float32)

def reference(queries, keys, values):
    first_pick, second_pick, scaling = tables(HD)
    shaped_q = jnp.transpose(queries.reshape(N_CHAIN, GROUP, HEADS, HD), (0, 2, 1, 3))
    shaped_k = jnp.transpose(keys.reshape(N_CHAIN, GROUP, HEADS, HD), (0, 2, 1, 3))
    shaped_v = jnp.transpose(values.reshape(N_CHAIN, GROUP, HEADS, HD), (0, 2, 1, 3))

    def head_state(pair):
        key_rows, value_rows = pair
        feats = expand(key_rows, first_pick, second_pick, scaling)
        return jnp.dot(feats.T, value_rows.astype(jnp.float32), precision=lax.Precision.HIGHEST)

    def head_read(pair):
        query_rows, state = pair
        feats = expand(query_rows, first_pick, second_pick, scaling)
        return jnp.dot(feats, state.astype(jnp.float32), precision=lax.Precision.HIGHEST)

    def step(prefix, inputs):
        index, query_group, key_group, value_group = inputs
        total = lax.map(head_state, (key_group, value_group))
        inclusive = prefix + total
        rounded = inclusive.astype(jnp.bfloat16)
        read = lax.map(head_read, (query_group, rounded))
        count = (index + 1).astype(jnp.float32) * GROUP
        result = (read / (HD * jnp.sqrt(count))).astype(jnp.bfloat16)
        return (inclusive, result)
    start = jnp.zeros((HEADS, F, HD), jnp.float32)
    order = jnp.arange(N_CHAIN, dtype=jnp.int32)
    _, outputs = lax.scan(step, start, (order, shaped_q, shaped_k, shaped_v))
    return jnp.transpose(outputs, (0, 2, 1, 3)).reshape(TOKENS, HEADS * HD)
```

```python
import functools

import jax
import jax.numpy as jnp
from jax import lax
from jax.experimental import pallas as pl
from jax.experimental.pallas import tpu as pltpu
from jax.sharding import Mesh
from jax.sharding import PartitionSpec as P

HD = 64
HEADS = 2
WIDE = HEADS * HD
BLOCK = 16
BLOCKS = HD // BLOCK
HALF = BLOCK // 2
PAIRS = [(a, b) for a in range(BLOCKS) for b in range(a + 1, BLOCKS)]
SAME = [(a, a) for a in range(BLOCKS)]
ROWS = (HALF + 1) * BLOCK * len(SAME) + BLOCK * BLOCK * len(PAIRS)

PLANE = ("pair", "core", "near", "row")
EVERY = ("depth",) + PLANE


def pieces():
    first = 0
    for turn in range(BLOCK):
        same = SAME if turn <= HALF else []
        yield turn, same, PAIRS, first
        first += BLOCK * (len(same) + len(PAIRS))


def turned(flat, plain, head, turn, lanes):
    out = []
    for block in range(BLOCKS):
        rows = pl.ds(head * HD + block * BLOCK, BLOCK)
        if turn == 0:
            out.append(plain[rows, lanes])
        else:
            out.append(pltpu.roll(flat[rows, lanes], BLOCK - turn, 0).astype(jnp.bfloat16))
    return out


def features(flat, plain, head, turn, pairs, lanes):
    second = turned(flat, plain, head, turn, lanes)
    first = [plain[pl.ds(head * HD + b * BLOCK, BLOCK), lanes] for b in range(BLOCKS)]
    return [first[a] * second[b] for a, b in pairs]


def state_kernel(keys, values, out, flat, plain):
    wide = keys[...].astype(jnp.float32).T
    flat[...] = wide
    plain[...] = wide.astype(jnp.bfloat16)
    lanes = pl.ds(0, keys.shape[0])
    left = lax.broadcasted_iota(jnp.int32, (1, WIDE), 1) < HD
    for turn, same, pairs, row in pieces():
        count = BLOCK * (len(same) + len(pairs))
        sums = []
        for head in range(HEADS):
            feats = jnp.concatenate(features(flat, plain, head, turn, same + pairs, lanes), 0)
            sums.append(jnp.dot(feats, values[...], preferred_element_type=jnp.float32))
        total = jnp.where(left, sums[0], sums[1])
        once = BLOCK * len(same) if turn in (0, HALF) else 0
        if once:
            out[pl.ds(row, once), :] = total[:once].astype(out.dtype)
        out[pl.ds(row + once, count - once), :] = (2.0 * total[once:]).astype(out.dtype)
    if out.shape[0] > ROWS:
        out[pl.ds(ROWS, out.shape[0] - ROWS), :] = jnp.zeros((out.shape[0] - ROWS, WIDE), out.dtype)


def read_kernel(tile, scale, queries, state, out, flat, plain, feats):
    turned_state = state[...].astype(jnp.float32).T.astype(jnp.bfloat16)
    wide = queries[...].astype(jnp.float32).T
    flat[...] = wide
    plain[...] = wide.astype(jnp.bfloat16)
    factor = scale[0]
    for step in range(queries.shape[0] // tile):
        lanes = pl.ds(step * tile, tile)
        both = []
        for head in range(HEADS):
            for turn, same, pairs, row in pieces():
                for k, block in enumerate(features(flat, plain, head, turn, same + pairs, lanes)):
                    feats[pl.ds(row + BLOCK * k, BLOCK), lanes] = block
            both.append(
                jnp.dot(
                    turned_state[head * HD : head * HD + HD, :ROWS],
                    feats[:, lanes],
                    preferred_element_type=jnp.float32,
                )
            )
        result = jnp.concatenate(both, 0) * factor
        out[lanes, :] = result.T.astype(out.dtype)


def in_vmem():
    return pl.BlockSpec(memory_space=pltpu.VMEM)


def make_state(keys, values, rows):
    tokens = keys.shape[0]
    return pl.pallas_call(
        state_kernel,
        out_shape=jax.ShapeDtypeStruct((rows, WIDE), jnp.bfloat16),
        in_specs=[in_vmem(), in_vmem()],
        out_specs=in_vmem(),
        scratch_shapes=[
            pltpu.VMEM((WIDE, tokens), jnp.float32),
            pltpu.VMEM((WIDE, tokens), jnp.bfloat16),
        ],
        compiler_params=pltpu.CompilerParams(vmem_limit_bytes=48 * 2**20),
        name="state",
    )(keys, values)


def read_state(scale, queries, state):
    tokens = queries.shape[0]
    return pl.pallas_call(
        functools.partial(read_kernel, min(512, tokens)),
        out_shape=jax.ShapeDtypeStruct((tokens, WIDE), jnp.bfloat16),
        in_specs=[pl.BlockSpec(memory_space=pltpu.SMEM), in_vmem(), in_vmem()],
        out_specs=in_vmem(),
        scratch_shapes=[
            pltpu.VMEM((WIDE, tokens), jnp.float32),
            pltpu.VMEM((WIDE, tokens), jnp.bfloat16),
            pltpu.VMEM((ROWS, tokens), jnp.bfloat16),
        ],
        compiler_params=pltpu.CompilerParams(vmem_limit_bytes=48 * 2**20),
        name="read",
    )(scale, queries, state)


def on_device(queries, keys, values):
    plane = lax.axis_size(PLANE)
    groups = lax.axis_size(("pair", "core"))
    shards = plane // groups
    part = -(-ROWS // (plane * 8)) * 8
    local = make_state(keys, values, plane * part).reshape(plane, part, WIDE)
    arrived = lax.all_to_all(local, PLANE, 0, 0, tiled=True)
    totals = jnp.sum(arrived.reshape(groups, shards, part, WIDE).astype(jnp.float32), 1)
    whole = jnp.sum(totals, 0)
    layers = lax.axis_size("depth")
    copies = jnp.broadcast_to(whole[None], (layers, part, WIDE))
    others = lax.all_to_all(copies, "depth", 0, 0, tiled=True)
    earlier = jnp.arange(layers) < lax.axis_index("depth")
    before = jnp.sum(jnp.where(earlier[:, None, None], others, 0.0), 0)
    running = []
    for group in range(groups):
        before = before + totals[group]
        running.append(before.astype(jnp.bfloat16))
    inclusive = jnp.stack(running)
    copies = jnp.broadcast_to(inclusive[:, None], (groups, shards, part, WIDE))
    state = lax.all_to_all(copies.reshape(plane, part, WIDE), PLANE, 0, 0, tiled=True)
    count = (lax.axis_index(("depth", "pair", "core")) + 1).astype(jnp.float32)
    scale = 1.0 / (HD * jnp.sqrt(count * (queries.shape[0] * shards)))
    return read_state(scale.reshape(1), queries, state.reshape(plane * part, WIDE))


def solution(mesh):
    torus = Mesh(mesh.devices.reshape(8, 2, 2, 2, 4), EVERY)
    spec = P(EVERY, None)
    return jax.shard_map(
        on_device, mesh=torus, in_specs=(spec, spec, spec), out_specs=spec, check_vma=False
    )
```

```python
import functools

import jax
import jax.numpy as jnp
from jax import lax
from jax.experimental import pallas as pl
from jax.experimental.pallas import tpu as pltpu
from jax.sharding import Mesh
from jax.sharding import PartitionSpec as P

HD = 64
HEADS = 2
WIDE = HEADS * HD
BLOCK = 16
BLOCKS = HD // BLOCK
HALF = BLOCK // 2
PAIRS = [(a, b) for a in range(BLOCKS) for b in range(a + 1, BLOCKS)]
SAME = [(a, a) for a in range(BLOCKS)]
ROWS = (HALF + 1) * BLOCK * len(SAME) + BLOCK * BLOCK * len(PAIRS)

CHUNKS = 4
TILE = 512

PLANE = ("pair", "core", "near", "row")
EVERY = ("depth",) + PLANE


def pieces():
    first = 0
    for turn in range(BLOCK):
        same = SAME if turn <= HALF else []
        yield turn, same, PAIRS, first
        first += BLOCK * (len(same) + len(PAIRS))


def turned(flat, plain, head, turn, lanes):
    out = []
    for block in range(BLOCKS):
        rows = pl.ds(head * HD + block * BLOCK, BLOCK)
        if turn == 0:
            out.append(plain[rows, lanes])
        else:
            out.append(pltpu.roll(flat[rows, lanes], BLOCK - turn, 0).astype(jnp.bfloat16))
    return out


def features(flat, plain, head, turn, pairs, lanes):
    second = turned(flat, plain, head, turn, lanes)
    first = [plain[pl.ds(head * HD + b * BLOCK, BLOCK), lanes] for b in range(BLOCKS)]
    return [first[a] * second[b] for a, b in pairs]


def state_kernel(keys_far, values_far, out_far, keys, values, flat, plain, out, arrived, left):
    tokens = keys.shape[0]
    piece = tokens // CHUNKS
    loads = []
    for k in range(CHUNKS):
        rows = pl.ds(k * piece, piece)
        loads.append(pltpu.make_async_copy(keys_far.at[rows], keys.at[rows], arrived.at[k]))
    loads.append(pltpu.make_async_copy(values_far, values, arrived.at[CHUNKS]))
    for load in loads:
        load.start()
    for k in range(CHUNKS):
        loads[k].wait()
        rows = pl.ds(k * piece, piece)
        wide = keys[rows, :].astype(jnp.float32).T
        flat[:, rows] = wide
        plain[:, rows] = wide.astype(jnp.bfloat16)
    loads[CHUNKS].wait()
    lanes = pl.ds(0, tokens)
    first_head = lax.broadcasted_iota(jnp.int32, (1, WIDE), 1) < HD
    stores, sent = [], 0
    for turn, same, pairs, row in pieces():
        count = BLOCK * (len(same) + len(pairs))
        sums = []
        for head in range(HEADS):
            feats = jnp.concatenate(features(flat, plain, head, turn, same + pairs, lanes), 0)
            sums.append(jnp.dot(feats, values[...], preferred_element_type=jnp.float32))
        total = jnp.where(first_head, sums[0], sums[1])
        once = BLOCK * len(same) if turn in (0, HALF) else 0
        if once:
            out[pl.ds(row, once), :] = total[:once].astype(out.dtype)
        out[pl.ds(row + once, count - once), :] = (2.0 * total[once:]).astype(out.dtype)
        done = row + count
        if turn == BLOCK - 1 and out.shape[0] > ROWS:
            out[pl.ds(ROWS, out.shape[0] - ROWS), :] = jnp.zeros((out.shape[0] - ROWS, WIDE), out.dtype)
            done = out.shape[0]
        if turn % 4 == 3:
            rows = pl.ds(sent, done - sent)
            stores.append(pltpu.make_async_copy(out.at[rows], out_far.at[rows], left.at[len(stores)]))
            stores[-1].start()
            sent = done
    for store in stores:
        store.wait()


def read_kernel(tile, scale, queries, state, out_far, out, flat, plain, feats, left):
    stores = []
    turned_state = state[...].astype(jnp.float32).T.astype(jnp.bfloat16)
    wide = queries[...].astype(jnp.float32).T
    flat[...] = wide
    plain[...] = wide.astype(jnp.bfloat16)
    factor = scale[0]
    for step in range(queries.shape[0] // tile):
        lanes = pl.ds(step * tile, tile)
        both = []
        for head in range(HEADS):
            for turn, same, pairs, row in pieces():
                for k, block in enumerate(features(flat, plain, head, turn, same + pairs, lanes)):
                    feats[pl.ds(row + BLOCK * k, BLOCK), lanes] = block
            both.append(
                jnp.dot(
                    turned_state[head * HD : head * HD + HD, :ROWS],
                    feats[:, lanes],
                    preferred_element_type=jnp.float32,
                )
            )
        result = jnp.concatenate(both, 0) * factor
        out[lanes, :] = result.T.astype(out.dtype)
        stores.append(pltpu.make_async_copy(out.at[lanes], out_far.at[lanes], left.at[step]))
        stores[-1].start()
    for store in stores:
        store.wait()


def in_vmem():
    return pl.BlockSpec(memory_space=pltpu.VMEM)


def in_hbm():
    return pl.BlockSpec(memory_space=pltpu.HBM)


def make_state(keys, values, rows):
    tokens = keys.shape[0]
    return pl.pallas_call(
        state_kernel,
        out_shape=jax.ShapeDtypeStruct((rows, WIDE), jnp.bfloat16),
        in_specs=[in_hbm(), in_hbm()],
        out_specs=in_hbm(),
        scratch_shapes=[
            pltpu.VMEM((tokens, WIDE), jnp.bfloat16),
            pltpu.VMEM((tokens, WIDE), jnp.bfloat16),
            pltpu.VMEM((WIDE, tokens), jnp.float32),
            pltpu.VMEM((WIDE, tokens), jnp.bfloat16),
            pltpu.VMEM((rows, WIDE), jnp.bfloat16),
            pltpu.SemaphoreType.DMA((CHUNKS + 1,)),
            pltpu.SemaphoreType.DMA((BLOCK // 4,)),
        ],
        compiler_params=pltpu.CompilerParams(vmem_limit_bytes=63 * 2**20),
        name="state",
    )(keys, values)


def read_state(scale, queries, state):
    tokens = queries.shape[0]
    tile = min(TILE, tokens)
    return pl.pallas_call(
        functools.partial(read_kernel, tile),
        out_shape=jax.ShapeDtypeStruct((tokens, WIDE), jnp.bfloat16),
        in_specs=[pl.BlockSpec(memory_space=pltpu.SMEM), in_vmem(), in_vmem()],
        out_specs=in_hbm(),
        scratch_shapes=[
            pltpu.VMEM((tokens, WIDE), jnp.bfloat16),
            pltpu.VMEM((WIDE, tokens), jnp.float32),
            pltpu.VMEM((WIDE, tokens), jnp.bfloat16),
            pltpu.VMEM((ROWS, tokens), jnp.bfloat16),
            pltpu.SemaphoreType.DMA((tokens // tile,)),
        ],
        compiler_params=pltpu.CompilerParams(vmem_limit_bytes=48 * 2**20),
        name="read",
    )(scale, queries, state)


def on_device(queries, keys, values):
    plane = lax.axis_size(PLANE)
    groups = lax.axis_size(("pair", "core"))
    shards = plane // groups
    part = -(-ROWS // (plane * 8)) * 8
    local = make_state(keys, values, plane * part).reshape(plane, part, WIDE)
    arrived = lax.all_to_all(local, PLANE, 0, 0, tiled=True)
    totals = jnp.sum(arrived.reshape(groups, shards, part, WIDE).astype(jnp.float32), 1)
    whole = jnp.sum(totals, 0).astype(jnp.bfloat16)
    layers = lax.axis_size("depth")
    copies = jnp.broadcast_to(whole[None], (layers, part, WIDE))
    others = lax.all_to_all(copies, "depth", 0, 0, tiled=True)
    earlier = jnp.arange(layers) < lax.axis_index("depth")
    before = jnp.sum(jnp.where(earlier[:, None, None], others.astype(jnp.float32), 0.0), 0)
    running = []
    for group in range(groups):
        before = before + totals[group]
        running.append(before.astype(jnp.bfloat16))
    inclusive = jnp.stack(running)
    copies = jnp.broadcast_to(inclusive[:, None], (groups, shards, part, WIDE))
    state = lax.all_to_all(copies.reshape(plane, part, WIDE), PLANE, 0, 0, tiled=True)
    count = (lax.axis_index(("depth", "pair", "core")) + 1).astype(jnp.float32)
    scale = 1.0 / (HD * jnp.sqrt(count * (queries.shape[0] * shards)))
    return read_state(scale.reshape(1), queries, state.reshape(plane * part, WIDE))


def solution(mesh):
    torus = Mesh(mesh.devices.reshape(8, 2, 2, 2, 4), EVERY)
    spec = P(EVERY, None)
    return jax.shard_map(
        on_device, mesh=torus, in_specs=(spec, spec, spec), out_specs=spec, check_vma=False
    )
```

```python
import functools

import jax
import jax.numpy as jnp
from jax import lax
from jax.experimental import pallas as pl
from jax.experimental.pallas import tpu as pltpu
from jax.sharding import Mesh
from jax.sharding import PartitionSpec as P

HD = 64
HEADS = 2
WIDE = HEADS * HD
BLOCK = 16
BAND = 2 * HD
ROWS = BLOCK * BAND + HD
CHUNK = 1024
TILE = 2048

PLANE = ("pair", "core", "near", "row")
EVERY = ("depth",) + PLANE


def band(flat, plain, head, s, lanes):
    rows = pl.ds(head * HD, HD)
    x = plain[rows, lanes]
    blocks = [plain[pl.ds(head * HD + k * BLOCK, BLOCK), lanes] for k in range(HD // BLOCK)]
    if s == BLOCK:
        return x * jnp.concatenate(blocks[2:] + blocks[:2], 0)
    lifted = jnp.concatenate(blocks[-1:] + blocks[:-1], 0)
    other = x
    if s:
        other = pltpu.roll(flat[rows, lanes], HD - s, 0).astype(jnp.bfloat16)
    return jnp.concatenate([x * other, lifted * other], 0)


def state_kernel(keys_far, values_far, out_far, keys, values, flat, plain, total, out, arrived, left):
    tokens = keys.shape[0]
    loads = []
    for k in range(tokens // CHUNK):
        rows = pl.ds(k * CHUNK, CHUNK)
        loads.append(pltpu.make_async_copy(keys_far.at[rows], keys.at[rows], arrived.at[2 * k]))
        loads.append(pltpu.make_async_copy(values_far.at[rows], values.at[rows], arrived.at[2 * k + 1]))
    for load in loads:
        load.start()
    padding = out.shape[0] - ROWS
    out[pl.ds(ROWS, padding), :] = jnp.zeros((padding, WIDE), out.dtype)
    first_head = lax.broadcasted_iota(jnp.int32, (1, WIDE), 1) < HD
    row = lax.broadcasted_iota(jnp.int32, (BAND, 1), 0)
    stores, sent = [], 0
    for k in range(tokens // CHUNK):
        last = k == tokens // CHUNK - 1
        lanes = pl.ds(k * CHUNK, CHUNK)
        loads[2 * k].wait()
        wide = keys[lanes, :].astype(jnp.float32).T
        flat[:, lanes] = wide
        plain[:, lanes] = wide.astype(jnp.bfloat16)
        loads[2 * k + 1].wait()
        for s in range(BLOCK + 1):
            sums = []
            for head in range(HEADS):
                feats = band(flat, plain, head, s, lanes)
                sums.append(jnp.dot(feats, values[lanes, :], preferred_element_type=jnp.float32))
            product = jnp.where(first_head, sums[0], sums[1])
            here = pl.ds(s * BAND, product.shape[0])
            if k:
                product = product + total[here, :]
            if not last:
                total[here, :] = product
                continue
            if s == 0:
                product = product * jnp.where(row < HD, 1.0, 2.0)
            elif s < BLOCK:
                product = product * 2.0
            out[here, :] = product.astype(out.dtype)
            if s % 4 == 3 or s == BLOCK:
                done = out.shape[0] if s == BLOCK else (s + 1) * BAND
                rows = pl.ds(sent, done - sent)
                stores.append(pltpu.make_async_copy(out.at[rows], out_far.at[rows], left.at[len(stores)]))
                stores[-1].start()
                sent = done
    for store in stores:
        store.wait()


def read_kernel(scale, queries, state, out_far, out, flat, plain, feats, left):
    turned = state[...].astype(jnp.float32).T.astype(jnp.bfloat16)
    wide = queries[...].astype(jnp.float32).T
    flat[...] = wide
    plain[...] = wide.astype(jnp.bfloat16)
    factor = scale[0]
    stores = []
    for step in range(out.shape[0] // TILE):
        lanes = pl.ds(step * TILE, TILE)
        both = []
        for head in range(HEADS):
            here = turned[head * HD : head * HD + HD, :ROWS]
            product = jnp.zeros((HD, TILE), jnp.float32)
            begin = 0
            for s in range(BLOCK + 1):
                value = band(flat, plain, head, s, lanes)
                feats[head, pl.ds(s * BAND, value.shape[0]), lanes] = value
                if s == BLOCK or s % 2 == 1 and s < BLOCK - 1:
                    end = s * BAND + value.shape[0]
                    product += jnp.dot(
                        here[:, begin:end],
                        feats[head, pl.ds(begin, end - begin), lanes],
                        preferred_element_type=jnp.float32,
                    )
                    begin = end
            both.append(product)
        result = jnp.concatenate(both, 0) * factor
        out[lanes, :] = result.T.astype(out.dtype)
        stores.append(pltpu.make_async_copy(out.at[lanes], out_far.at[lanes], left.at[step]))
        stores[-1].start()
    for store in stores:
        store.wait()


def in_vmem():
    return pl.BlockSpec(memory_space=pltpu.VMEM)


def in_hbm():
    return pl.BlockSpec(memory_space=pltpu.HBM)


def make_state(keys, values, rows):
    tokens = keys.shape[0]
    return pl.pallas_call(
        state_kernel,
        out_shape=jax.ShapeDtypeStruct((rows, WIDE), jnp.bfloat16),
        in_specs=[in_hbm(), in_hbm()],
        out_specs=in_hbm(),
        scratch_shapes=[
            pltpu.VMEM((tokens, WIDE), jnp.bfloat16),
            pltpu.VMEM((tokens, WIDE), jnp.bfloat16),
            pltpu.VMEM((WIDE, tokens), jnp.float32),
            pltpu.VMEM((WIDE, tokens), jnp.bfloat16),
            pltpu.VMEM((ROWS, WIDE), jnp.float32),
            pltpu.VMEM((rows, WIDE), jnp.bfloat16),
            pltpu.SemaphoreType.DMA((2 * tokens // CHUNK,)),
            pltpu.SemaphoreType.DMA((BLOCK // 4 + 1,)),
        ],
        compiler_params=pltpu.CompilerParams(vmem_limit_bytes=62 * 2**20),
        name="state",
    )(keys, values)


def read_state(scale, queries, state):
    tokens = queries.shape[0]
    return pl.pallas_call(
        read_kernel,
        out_shape=jax.ShapeDtypeStruct((tokens, WIDE), jnp.bfloat16),
        in_specs=[pl.BlockSpec(memory_space=pltpu.SMEM), in_vmem(), in_vmem()],
        out_specs=in_hbm(),
        scratch_shapes=[
            pltpu.VMEM((tokens, WIDE), jnp.bfloat16),
            pltpu.VMEM((WIDE, tokens), jnp.float32),
            pltpu.VMEM((WIDE, tokens), jnp.bfloat16),
            pltpu.VMEM((HEADS, ROWS, tokens), jnp.bfloat16),
            pltpu.SemaphoreType.DMA((tokens // TILE,)),
        ],
        compiler_params=pltpu.CompilerParams(vmem_limit_bytes=48 * 2**20),
        name="read",
    )(scale, queries, state)


def on_device(queries, keys, values):
    plane = lax.axis_size(PLANE)
    groups = lax.axis_size(("pair", "core"))
    shards = plane // groups
    part = (-(-ROWS // (plane * 8)) * 8, WIDE)
    local = make_state(keys, values, plane * part[0]).reshape(plane, *part)
    arrived = lax.all_to_all(local, PLANE, 0, 0, tiled=True)
    totals = jnp.sum(arrived.reshape(groups, shards, *part).astype(jnp.float32), 1)
    whole = jnp.sum(totals, 0).astype(jnp.bfloat16)
    layers = lax.axis_size("depth")
    copies = jnp.broadcast_to(whole[None], (layers, *part))
    others = lax.all_to_all(copies, "depth", 0, 0, tiled=True)
    earlier = jnp.arange(layers) < lax.axis_index("depth")
    before = jnp.sum(jnp.where(earlier[:, None, None], others.astype(jnp.float32), 0.0), 0)
    running = []
    for group in range(groups):
        before = before + totals[group]
        running.append(before.astype(jnp.bfloat16))
    inclusive = jnp.stack(running)
    copies = jnp.broadcast_to(inclusive[:, None], (groups, shards, *part))
    state = lax.all_to_all(copies.reshape(plane, *part), PLANE, 0, 0, tiled=True)
    count = (lax.axis_index(("depth", "pair", "core")) + 1).astype(jnp.float32)
    scale = 1.0 / (HD * jnp.sqrt(count * (queries.shape[0] * shards)))
    return read_state(scale.reshape(1), queries, state.reshape(-1, WIDE))


def solution(mesh):
    torus = Mesh(mesh.devices.reshape(8, 2, 2, 2, 4), EVERY)
    spec = P(EVERY, None)
    return jax.shard_map(
        on_device, mesh=torus, in_specs=(spec, spec, spec), out_specs=spec, check_vma=False
    )
```

```python
import functools

import jax
import jax.numpy as jnp
from jax import lax
from jax.experimental import pallas as pl
from jax.experimental.pallas import tpu as pltpu
from jax.sharding import Mesh
from jax.sharding import PartitionSpec as P

HD = 64
HEADS = 2
WIDE = HEADS * HD
BLOCK = 16
BAND = 2 * HD
ROWS = BLOCK * BAND + HD
CHUNK = 1024
TILE = 2048

PLANE = ("pair", "core", "near", "row")
EVERY = ("depth",) + PLANE


def band(flat, plain, head, s, lanes):
    rows = pl.ds(head * HD, HD)
    x = plain[rows, lanes]
    blocks = [plain[pl.ds(head * HD + k * BLOCK, BLOCK), lanes] for k in range(HD // BLOCK)]
    if s == BLOCK:
        return x * jnp.concatenate(blocks[2:] + blocks[:2], 0)
    lifted = jnp.concatenate(blocks[-1:] + blocks[:-1], 0)
    other = x
    if s:
        other = pltpu.roll(flat[rows, lanes], HD - s, 0).astype(jnp.bfloat16)
    return jnp.concatenate([x * other, lifted * other], 0)


def state_kernel(keys_far, values_far, out_far, keys, values, flat, plain, total, out, arrived, left):
    tokens = keys.shape[0]
    loads = []
    for k in range(tokens // CHUNK):
        rows = pl.ds(k * CHUNK, CHUNK)
        loads.append(pltpu.make_async_copy(keys_far.at[rows], keys.at[rows], arrived.at[2 * k]))
        loads.append(pltpu.make_async_copy(values_far.at[rows], values.at[rows], arrived.at[2 * k + 1]))
    for load in loads:
        load.start()
    padding = out.shape[0] - ROWS
    out[pl.ds(ROWS, padding), :] = jnp.zeros((padding, WIDE), out.dtype)
    first_head = lax.broadcasted_iota(jnp.int32, (1, WIDE), 1) < HD
    row = lax.broadcasted_iota(jnp.int32, (BAND, 1), 0)
    stores, sent = [], 0
    for k in range(tokens // CHUNK):
        last = k == tokens // CHUNK - 1
        lanes = pl.ds(k * CHUNK, CHUNK)
        loads[2 * k].wait()
        wide = keys[lanes, :].astype(jnp.float32).T
        flat[:, lanes] = wide
        plain[:, lanes] = wide.astype(jnp.bfloat16)
        loads[2 * k + 1].wait()
        for s in range(BLOCK + 1):
            sums = []
            for head in range(HEADS):
                feats = band(flat, plain, head, s, lanes)
                sums.append(jnp.dot(feats, values[lanes, :], preferred_element_type=jnp.float32))
            product = jnp.where(first_head, sums[0], sums[1])
            here = pl.ds(s * BAND, product.shape[0])
            if k:
                product = product + total[here, :]
            if not last:
                total[here, :] = product
                continue
            if s == 0:
                product = product * jnp.where(row < HD, 1.0, 2.0)
            elif s < BLOCK:
                product = product * 2.0
            out[here, :] = product.astype(out.dtype)
            if s % 4 == 3 or s == BLOCK:
                done = out.shape[0] if s == BLOCK else (s + 1) * BAND
                rows = pl.ds(sent, done - sent)
                stores.append(pltpu.make_async_copy(out.at[rows], out_far.at[rows], left.at[len(stores)]))
                stores[-1].start()
                sent = done
    for store in stores:
        store.wait()


def read_kernel(scale, queries, state, out_far, out, flat, plain, feats, left):
    turned = state[...].astype(jnp.float32).T.astype(jnp.bfloat16)
    wide = queries[...].astype(jnp.float32).T
    flat[...] = wide
    plain[...] = wide.astype(jnp.bfloat16)
    factor = scale[0]
    stores = []
    for step in range(out.shape[0] // TILE):
        lanes = pl.ds(step * TILE, TILE)
        both = []
        for head in range(HEADS):
            here = turned[head * HD : head * HD + HD, :ROWS]
            product = jnp.zeros((HD, TILE), jnp.float32)
            begin = 0
            for s in range(BLOCK + 1):
                value = band(flat, plain, head, s, lanes)
                feats[head, pl.ds(s * BAND, value.shape[0]), lanes] = value
                if s == BLOCK or s % 2 == 1 and s < BLOCK - 1:
                    end = s * BAND + value.shape[0]
                    product += jnp.dot(
                        here[:, begin:end],
                        feats[head, pl.ds(begin, end - begin), lanes],
                        preferred_element_type=jnp.float32,
                    )
                    begin = end
            both.append(product)
        result = jnp.concatenate(both, 0) * factor
        out[lanes, :] = result.T.astype(out.dtype)
        stores.append(pltpu.make_async_copy(out.at[lanes], out_far.at[lanes], left.at[step]))
        stores[-1].start()
    for store in stores:
        store.wait()


def in_vmem():
    return pl.BlockSpec(memory_space=pltpu.VMEM)


def in_hbm():
    return pl.BlockSpec(memory_space=pltpu.HBM)


def make_state(keys, values, rows):
    tokens = keys.shape[0]
    return pl.pallas_call(
        state_kernel,
        out_shape=jax.ShapeDtypeStruct((rows, WIDE), jnp.bfloat16),
        in_specs=[in_hbm(), in_hbm()],
        out_specs=in_hbm(),
        scratch_shapes=[
            pltpu.VMEM((tokens, WIDE), jnp.bfloat16),
            pltpu.VMEM((tokens, WIDE), jnp.bfloat16),
            pltpu.VMEM((WIDE, tokens), jnp.float32),
            pltpu.VMEM((WIDE, tokens), jnp.bfloat16),
            pltpu.VMEM((ROWS, WIDE), jnp.float32),
            pltpu.VMEM((rows, WIDE), jnp.bfloat16),
            pltpu.SemaphoreType.DMA((2 * tokens // CHUNK,)),
            pltpu.SemaphoreType.DMA((BLOCK // 4 + 1,)),
        ],
        compiler_params=pltpu.CompilerParams(vmem_limit_bytes=62 * 2**20),
        name="state",
    )(keys, values)


def read_state(scale, queries, state):
    tokens = queries.shape[0]
    return pl.pallas_call(
        read_kernel,
        out_shape=jax.ShapeDtypeStruct((tokens, WIDE), jnp.bfloat16),
        in_specs=[pl.BlockSpec(memory_space=pltpu.SMEM), in_vmem(), in_vmem()],
        out_specs=in_hbm(),
        scratch_shapes=[
            pltpu.VMEM((tokens, WIDE), jnp.bfloat16),
            pltpu.VMEM((WIDE, tokens), jnp.float32),
            pltpu.VMEM((WIDE, tokens), jnp.bfloat16),
            pltpu.VMEM((HEADS, ROWS, tokens), jnp.bfloat16),
            pltpu.SemaphoreType.DMA((tokens // TILE,)),
        ],
        compiler_params=pltpu.CompilerParams(vmem_limit_bytes=48 * 2**20),
        name="read",
    )(scale, queries, state)


def on_device(queries, keys, values):
    plane = lax.axis_size(PLANE)
    groups = lax.axis_size(("pair", "core"))
    shards = plane // groups
    layers = lax.axis_size("depth")
    part = (-(-ROWS // (plane * 8)) * 8, WIDE)
    count = (lax.axis_index(("depth", "pair", "core")) + 1).astype(jnp.float32)
    scale = (1.0 / (HD * jnp.sqrt(count * (queries.shape[0] * shards)))).reshape(1)
    earlier = (jnp.arange(layers) < lax.axis_index("depth")).astype(jnp.float32)
    local = make_state(keys, values, plane * part[0]).reshape(plane, *part)
    local, earlier, scale = lax.optimization_barrier((local, earlier, scale))
    arrived = lax.all_to_all(local, PLANE, 0, 0, tiled=True)
    totals = jnp.sum(arrived.reshape(groups, shards, *part).astype(jnp.float32), 1)
    whole = jnp.sum(totals, 0).astype(jnp.bfloat16)
    copies = jnp.broadcast_to(whole[None], (layers, *part))
    copies, totals, earlier, scale = lax.optimization_barrier((copies, totals, earlier, scale))
    others = lax.all_to_all(copies, "depth", 0, 0, tiled=True)
    before = jnp.sum(others.astype(jnp.float32) * earlier[:, None, None], 0)
    running = []
    for group in range(groups):
        before = before + totals[group]
        running.append(before.astype(jnp.bfloat16))
    inclusive = jnp.stack(running)
    copies = jnp.broadcast_to(inclusive[:, None], (groups, shards, *part))
    copies, scale = lax.optimization_barrier((copies.reshape(plane, *part), scale))
    state = lax.all_to_all(copies, PLANE, 0, 0, tiled=True)
    state, scale = lax.optimization_barrier((state, scale))
    return read_state(scale, queries, state.reshape(-1, WIDE))


def solution(mesh):
    torus = Mesh(mesh.devices.reshape(8, 2, 2, 2, 4), EVERY)
    spec = P(EVERY, None)
    return jax.shard_map(
        on_device, mesh=torus, in_specs=(spec, spec, spec), out_specs=spec, check_vma=False
    )
```

```python
import jax
import jax.numpy as jnp
import numpy as np
from jax import lax
from jax.experimental import pallas as pl
from jax.experimental.pallas import tpu as pltpu
from jax.sharding import Mesh
from jax.sharding import PartitionSpec as P

HD = 64
HEADS = 2
WIDE = HEADS * HD
BLOCK = 16
BLOCKS = HD // BLOCK
BAND = 2 * HD
ROWS = BLOCK * BAND + HD
STRIP = 9
STRIPS = 4
TALL = 8
PARTS = STRIPS * HD // TALL

DEPTH = ("depth_0", "depth_1", "depth_2")
PLANE = ("pair", "core", "near", "row")
EVERY = DEPTH + PLANE


def head_blocks(wide, step):
    rows = [HD * head + BLOCK * ((k + step) % BLOCKS) for head in range(HEADS) for k in range(BLOCKS)]
    return jnp.concatenate([wide[row : row + BLOCK] for row in rows], 0)


def state_kernel(keys_far, values_far, out_far, keys, values, out, arrived, left):
    loads = [
        pltpu.make_async_copy(keys_far, keys, arrived.at[0]),
        pltpu.make_async_copy(values_far, values, arrived.at[1]),
    ]
    for load in loads:
        load.start()
    filled = (2 * BLOCK + 1) % STRIP * WIDE
    for k in range(HD // TALL):
        rest = out.shape[2] - filled
        out[PARTS - HD // TALL + k, :, pl.ds(filled, rest)] = jnp.zeros((TALL, rest), out.dtype)
    loads[0].wait()
    x = keys[...]
    wide = x.astype(jnp.float32).T
    lifted = head_blocks(wide, -1).astype(jnp.bfloat16).T
    loads[1].wait()
    turned_values = values[...].astype(jnp.float32).T.astype(jnp.bfloat16)
    lane = lax.broadcasted_iota(jnp.int32, (1, WIDE), 1)
    stores = []
    for s in range(BLOCK + 1):
        if s == 0:
            other = x
        elif s == BLOCK:
            other = head_blocks(wide, 2).astype(jnp.bfloat16).T
        else:
            heads = [pltpu.roll(wide[HD * head : HD * head + HD], HD - s, 0) for head in range(HEADS)]
            other = jnp.concatenate(heads, 0).astype(jnp.bfloat16).T
        feats = x * other if s == BLOCK else jnp.concatenate([x * other, lifted * other], 1)
        product = jnp.dot(turned_values, feats, preferred_element_type=jnp.float32)
        for half in range(feats.shape[1] // WIDE):
            piece = product[:, WIDE * half : WIDE * half + WIDE]
            piece = jnp.where(lane < HD, piece[:HD], piece[HD:])
            if s < BLOCK and (s or half):
                piece = 2.0 * piece
            strip, place = divmod(2 * s + half, STRIP)
            for k in range(HD // TALL):
                part = piece[TALL * k : TALL * k + TALL].astype(out.dtype)
                out[HD // TALL * strip + k, :, pl.ds(WIDE * place, WIDE)] = part
            if place == STRIP - 1 or s == BLOCK:
                parts = pl.ds(HD // TALL * strip, HD // TALL)
                stores.append(pltpu.make_async_copy(out.at[parts], out_far.at[parts], left.at[strip]))
                stores[-1].start()
    for store in stores:
        store.wait()


def band(flat, plain, head, s):
    x = plain[pl.ds(head * HD, HD), :]
    blocks = [plain[pl.ds(head * HD + k * BLOCK, BLOCK), :] for k in range(BLOCKS)]
    if s == BLOCK:
        return x * jnp.concatenate(blocks[2:] + blocks[:2], 0)
    lifted = jnp.concatenate(blocks[-1:] + blocks[:-1], 0)
    other = x
    if s:
        other = pltpu.roll(flat[pl.ds(head * HD, HD), :], HD - s, 0).astype(jnp.bfloat16)
    return jnp.concatenate([x * other, lifted * other], 0)


def state_band(whole, head, s):
    lane = lax.broadcasted_iota(jnp.int32, (1, WIDE), 1)
    low = whole[:, pl.ds(2 * s * WIDE, WIDE)]
    if head == 1:
        low = pltpu.roll(low, HD, 1)
    if s == BLOCK:
        return low[:, :HD].astype(jnp.bfloat16)
    high = whole[:, pl.ds(2 * s * WIDE + WIDE, WIDE)]
    if head == 0:
        high = pltpu.roll(high, HD, 1)
    return jnp.where(lane < HD, low, high).astype(jnp.bfloat16)


def read_kernel(scale, queries, state, out, flat, plain, feats, whole):
    for k in range(PARTS):
        strip, rows = divmod(k, HD // TALL)
        lanes = pl.ds(STRIP * WIDE * strip, STRIP * WIDE)
        whole[pl.ds(TALL * rows, TALL), lanes] = state[k].astype(jnp.float32)
    wide = queries[...].astype(jnp.float32).T
    flat[...] = wide
    plain[...] = wide.astype(jnp.bfloat16)
    both = []
    for head in range(HEADS):
        product = jnp.zeros((HD, queries.shape[0]), jnp.float32)
        begin, left = 0, []
        for s in range(BLOCK + 1):
            value = band(flat, plain, head, s)
            end = s * BAND + value.shape[0]
            feats[head, pl.ds(s * BAND, value.shape[0]), :] = value
            left.append(state_band(whole, head, s))
            if s == BLOCK or s % 2 == 1 and s < BLOCK - 1:
                right = feats[head, pl.ds(begin, end - begin), :]
                product += jnp.dot(jnp.concatenate(left, 1), right, preferred_element_type=jnp.float32)
                begin, left = end, []
        both.append(product)
    result = jnp.concatenate(both, 0) * scale[0]
    out[...] = result.T.astype(out.dtype)


def in_vmem():
    return pl.BlockSpec(memory_space=pltpu.VMEM)


def in_hbm():
    return pl.BlockSpec(memory_space=pltpu.HBM)


def make_state(keys, values):
    tokens = keys.shape[0]
    part = (TALL, STRIP * WIDE)
    return pl.pallas_call(
        state_kernel,
        out_shape=jax.ShapeDtypeStruct((PARTS, *part), jnp.bfloat16),
        in_specs=[in_hbm(), in_hbm()],
        out_specs=in_hbm(),
        scratch_shapes=[
            pltpu.VMEM((tokens, WIDE), jnp.bfloat16),
            pltpu.VMEM((tokens, WIDE), jnp.bfloat16),
            pltpu.VMEM((PARTS, *part), jnp.bfloat16),
            pltpu.SemaphoreType.DMA((2,)),
            pltpu.SemaphoreType.DMA((STRIPS,)),
        ],
        compiler_params=pltpu.CompilerParams(vmem_limit_bytes=62 * 2**20),
        name="state",
    )(keys, values)


def read_state(scale, queries, state):
    tokens = queries.shape[0]
    return pl.pallas_call(
        read_kernel,
        out_shape=jax.ShapeDtypeStruct((tokens, WIDE), jnp.bfloat16),
        in_specs=[pl.BlockSpec(memory_space=pltpu.SMEM), in_vmem(), in_vmem()],
        out_specs=in_vmem(),
        scratch_shapes=[
            pltpu.VMEM((WIDE, tokens), jnp.float32),
            pltpu.VMEM((WIDE, tokens), jnp.bfloat16),
            pltpu.VMEM((HEADS, ROWS, tokens), jnp.bfloat16),
            pltpu.VMEM((HD, STRIPS * STRIP * WIDE), jnp.float32),
        ],
        compiler_params=pltpu.CompilerParams(vmem_limit_bytes=48 * 2**20),
        name="read",
    )(scale, queries, state)


def on_device(queries, keys, values):
    plane = lax.axis_size(PLANE)
    groups = lax.axis_size(("pair", "core"))
    shards = plane // groups
    layers = lax.axis_size(DEPTH)
    count = (lax.axis_index(DEPTH + ("pair", "core")) + 1).astype(jnp.float32)
    scale = (1.0 / (HD * jnp.sqrt(count * (queries.shape[0] * shards)))).reshape(1)
    order = np.arange(layers).reshape([lax.axis_size(axis) for axis in DEPTH]).T.reshape(-1)
    earlier = (jnp.asarray(order) < lax.axis_index(DEPTH)).astype(jnp.float32)
    local = make_state(keys, values)
    part = local.shape[1:]
    local, earlier, scale = lax.optimization_barrier((local, earlier, scale))
    arrived = lax.all_to_all(local, PLANE, 0, 0, tiled=True)
    totals = jnp.sum(arrived.reshape(groups, shards, *part).astype(jnp.float32), 1)
    whole = jnp.sum(totals, 0).astype(jnp.bfloat16)
    copies = jnp.broadcast_to(whole[None], (layers, *part))
    copies, totals, earlier, scale = lax.optimization_barrier((copies, totals, earlier, scale))
    others = lax.all_to_all(copies, DEPTH[::-1], 0, 0, tiled=True)
    before = jnp.sum(others.astype(jnp.float32) * earlier[:, None, None], 0)
    running = []
    for group in range(groups):
        before = before + totals[group]
        running.append(before.astype(jnp.bfloat16))
    inclusive = jnp.stack(running)
    copies = jnp.broadcast_to(inclusive[:, None], (groups, shards, *part))
    copies, scale = lax.optimization_barrier((copies.reshape(plane, *part), scale))
    state = lax.all_to_all(copies, PLANE, 0, 0, tiled=True)
    state, scale = lax.optimization_barrier((state, scale))
    return read_state(scale, queries, state)


def solution(mesh):
    torus = Mesh(mesh.devices.reshape(2, 2, 2, 2, 2, 2, 4), EVERY)
    spec = P(EVERY, None)
    return jax.shard_map(
        on_device, mesh=torus, in_specs=(spec, spec, spec), out_specs=spec, check_vma=False
    )
```

```python
import jax
import jax.numpy as jnp
from jax import lax
from jax.experimental import pallas as pl
from jax.experimental.pallas import tpu as pltpu
from jax.sharding import Mesh
from jax.sharding import PartitionSpec as P

HD = 64
HEADS = 2
WIDE = HEADS * HD
BLOCK = 16
BLOCKS = HD // BLOCK
TURNS = BLOCK // 2
BAND = 2 * HD
ROWS = 2 * TURNS * BAND + HD
STRIP = 9
TALL = 8
PARTS = 2 * WIDE // TALL

DEPTH = ("depth_0", "depth_1", "depth_2")
PLANE = ("pair", "core", "near", "row")
EVERY = DEPTH + PLANE


def across(wide, swap, move=0, turn=0):
    rows = []
    for head in (1, 0) if swap else (0, 1):
        mine = wide[HD * head : HD * head + HD]
        if move:
            mine = jnp.concatenate([mine[BLOCK * (move % BLOCKS) :], mine[: BLOCK * (move % BLOCKS)]], 0)
        if turn:
            mine = pltpu.roll(mine, HD - turn, 0)
        rows.append(mine)
    return jnp.concatenate(rows, 0).astype(jnp.bfloat16).T


def state_kernel(keys_far, values_far, out_far, keys, values, out, arrived, left):
    loads = [
        pltpu.make_async_copy(keys_far, keys, arrived.at[0]),
        pltpu.make_async_copy(values_far, values, arrived.at[1]),
    ]
    for load in loads:
        load.start()
    stores = []

    def store(strip, begin, end):
        parts = pl.ds(WIDE // TALL * strip, WIDE // TALL)
        lanes = pl.ds(BAND * begin, BAND * (end - begin))
        stores.append(
            pltpu.make_async_copy(out.at[parts, :, lanes], out_far.at[parts, :, lanes], left.at[len(stores)])
        )
        stores[-1].start()

    def put(place, heads):
        strip, place = divmod(place, STRIP)
        for k in range(WIDE // TALL):
            head, row = divmod(k * TALL, HD)
            part = heads[head][row : row + TALL].astype(out.dtype)
            out[WIDE // TALL * strip + k, :, pl.ds(BAND * place, BAND)] = part

    loads[0].wait()
    x = keys[...]
    wide = x.astype(jnp.float32).T
    first = [x, across(wide, False, -1)], [across(wide, True), across(wide, True, -1)]
    loads[1].wait()
    turned_values = values[...].astype(jnp.float32).T.astype(jnp.bfloat16)
    lane = lax.broadcasted_iota(jnp.int32, (1, BAND), 1)
    for s in range(TURNS):
        others = across(wide, False, 0, s) if s else x, across(wide, True, 0, s + TURNS)
        feats = jnp.concatenate([first[swap][k] * others[swap] for k in range(2) for swap in range(2)], 1)
        product = jnp.dot(turned_values, feats, preferred_element_type=jnp.float32)
        for k in range(2):
            plain, swapped = (product[:, BAND * j : BAND * j + BAND] for j in (2 * k, 2 * k + 1))
            heads = [
                jnp.where(lane < HD, plain[:HD], swapped[:HD]),
                jnp.where(lane < HD, swapped[HD:], plain[HD:]),
            ]
            for head in range(HEADS):
                once = (lane < HD) == (head == 0) if s == 0 and k == 0 else lane < 0
                heads[head] = heads[head] * jnp.where(once, 1.0, 2.0)
            put(2 * s + k, heads)
        if 2 * s + 2 == STRIP + 1:
            store(0, 0, STRIP)
        if s == TURNS - 2:
            store(1, 0, 2 * s + 2 - STRIP)
    feats = jnp.concatenate([first[swap][0] * across(wide, swap == 1, 2) for swap in range(2)], 1)
    product = jnp.dot(turned_values, feats, preferred_element_type=jnp.float32)
    heads = []
    for head in range(HEADS):
        mine = product[HD * head : HD * head + HD, BAND * head : BAND * head + BAND]
        heads.append(jnp.where(lane < HD, mine, 0.0))
    put(2 * TURNS, heads)
    put(2 * TURNS + 1, [jnp.zeros((HD, BAND), jnp.float32)] * HEADS)
    store(1, 2 * TURNS - 2 - STRIP, STRIP)
    for copy in stores:
        copy.wait()


def query_band(flat, plain, head, s):
    rows = pl.ds(head * HD, HD)
    x = plain[rows, :]
    blocks = [plain[pl.ds(head * HD + k * BLOCK, BLOCK), :] for k in range(BLOCKS)]
    if s == TURNS:
        return x * jnp.concatenate(blocks[2:] + blocks[:2], 0)
    lifted = jnp.concatenate(blocks[-1:] + blocks[:-1], 0)
    turns = (s, s + TURNS) if head == 0 else (s + TURNS, s)
    others = [pltpu.roll(flat[rows, :], HD - t, 0).astype(jnp.bfloat16) if t else x for t in turns]
    return jnp.concatenate([first * other for first in (x, lifted) for other in others], 0)


def read_kernel(scale, queries, state, out, flat, plain, feats, whole):
    for k in range(PARTS):
        strip, rows = divmod(k, WIDE // TALL)
        whole[pl.ds(TALL * rows, TALL), pl.ds(STRIP * BAND * strip, STRIP * BAND)] = state[k].astype(jnp.float32)
    wide = queries[...].astype(jnp.float32).T
    flat[...] = wide
    plain[...] = wide.astype(jnp.bfloat16)
    both = []
    for head in range(HEADS):
        product = jnp.zeros((HD, queries.shape[0]), jnp.float32)
        begin = 0
        for s in range(TURNS + 1):
            value = query_band(flat, plain, head, s)
            end = 2 * s * BAND + value.shape[0]
            feats[head, pl.ds(2 * s * BAND, value.shape[0]), :] = value
            if s != TURNS - 1:
                here = whole[pl.ds(head * HD, HD), :][:, begin:end].astype(jnp.bfloat16)
                right = feats[head, pl.ds(begin, end - begin), :]
                product += jnp.dot(here, right, preferred_element_type=jnp.float32)
                begin = end
        both.append(product)
    result = jnp.concatenate(both, 0) * scale[0]
    out[...] = result.T.astype(out.dtype)


def in_vmem():
    return pl.BlockSpec(memory_space=pltpu.VMEM)


def in_hbm():
    return pl.BlockSpec(memory_space=pltpu.HBM)


def make_state(keys, values):
    tokens = keys.shape[0]
    part = (TALL, STRIP * BAND)
    return pl.pallas_call(
        state_kernel,
        out_shape=jax.ShapeDtypeStruct((PARTS, *part), jnp.bfloat16),
        in_specs=[in_hbm(), in_hbm()],
        out_specs=in_hbm(),
        scratch_shapes=[
            pltpu.VMEM((tokens, WIDE), jnp.bfloat16),
            pltpu.VMEM((tokens, WIDE), jnp.bfloat16),
            pltpu.VMEM((PARTS, *part), jnp.bfloat16),
            pltpu.SemaphoreType.DMA((2,)),
            pltpu.SemaphoreType.DMA((3,)),
        ],
        compiler_params=pltpu.CompilerParams(vmem_limit_bytes=62 * 2**20),
        name="state",
    )(keys, values)


def read_state(scale, queries, state):
    tokens = queries.shape[0]
    return pl.pallas_call(
        read_kernel,
        out_shape=jax.ShapeDtypeStruct((tokens, WIDE), jnp.bfloat16),
        in_specs=[pl.BlockSpec(memory_space=pltpu.SMEM), in_vmem(), in_vmem()],
        out_specs=in_vmem(),
        scratch_shapes=[
            pltpu.VMEM((WIDE, tokens), jnp.float32),
            pltpu.VMEM((WIDE, tokens), jnp.bfloat16),
            pltpu.VMEM((HEADS, ROWS, tokens), jnp.bfloat16),
            pltpu.VMEM((WIDE, 2 * STRIP * BAND), jnp.float32),
        ],
        compiler_params=pltpu.CompilerParams(vmem_limit_bytes=48 * 2**20),
        name="read",
    )(scale, queries, state)


def on_device(queries, keys, values):
    plane = lax.axis_size(PLANE)
    groups = lax.axis_size(("pair", "core"))
    shards = plane // groups
    layers = lax.axis_size(DEPTH)
    count = (lax.axis_index(DEPTH + ("pair", "core")) + 1).astype(jnp.float32)
    scale = (1.0 / (HD * jnp.sqrt(count * (queries.shape[0] * shards)))).reshape(1)
    order, place = 0, lax.iota(jnp.int32, layers)
    for axis in DEPTH:
        size = lax.axis_size(axis)
        order, place = order * size + place % size, place // size
    earlier = (order < lax.axis_index(DEPTH)).astype(jnp.float32)
    local = make_state(keys, values)
    part = local.shape[1:]
    local, earlier, scale = lax.optimization_barrier((local, earlier, scale))
    arrived = lax.all_to_all(local, PLANE, 0, 0, tiled=True)
    totals = jnp.sum(arrived.reshape(groups, shards, *part).astype(jnp.float32), 1)
    whole = jnp.sum(totals, 0).astype(jnp.bfloat16)
    copies = jnp.broadcast_to(whole[None], (layers, *part))
    copies, totals, earlier, scale = lax.optimization_barrier((copies, totals, earlier, scale))
    others = lax.all_to_all(copies, DEPTH[::-1], 0, 0, tiled=True)
    before = jnp.sum(others.astype(jnp.float32) * earlier[:, None, None], 0)
    running = []
    for group in range(groups):
        before = before + totals[group]
        running.append(before.astype(jnp.bfloat16))
    inclusive = jnp.stack(running)
    copies = jnp.broadcast_to(inclusive[:, None], (groups, shards, *part))
    copies, scale = lax.optimization_barrier((copies.reshape(plane, *part), scale))
    state = lax.all_to_all(copies, PLANE, 0, 0, tiled=True)
    state, scale = lax.optimization_barrier((state, scale))
    return read_state(scale, queries, state)


def solution(mesh):
    torus = Mesh(mesh.devices.reshape(2, 2, 2, 2, 2, 2, 4), EVERY)
    spec = P(EVERY, None)
    return jax.shard_map(
        on_device, mesh=torus, in_specs=(spec, spec, spec), out_specs=spec, check_vma=False
    )
```

```python
import jax
import jax.numpy as jnp
from jax import lax
from jax.experimental import pallas as pl
from jax.experimental.pallas import tpu as pltpu
from jax.sharding import Mesh
from jax.sharding import PartitionSpec as P

HD = 64
HEADS = 2
WIDE = HEADS * HD
BLOCK = 16
BLOCKS = HD // BLOCK
TURNS = BLOCK // 2
BAND = 2 * HD
ROWS = 2 * TURNS * BAND + HD
STRIP = 9
TALL = 8
READS = 2
PARTS = 2 * WIDE // TALL

DEPTH = ("depth_0", "depth_1", "depth_2")
PLANE = ("pair", "core", "near", "row")
EVERY = DEPTH + PLANE


def across(wide, swap, move=0, turn=0):
    rows = []
    for head in (1, 0) if swap else (0, 1):
        mine = wide[HD * head : HD * head + HD]
        if move:
            mine = jnp.concatenate([mine[BLOCK * (move % BLOCKS) :], mine[: BLOCK * (move % BLOCKS)]], 0)
        if turn:
            mine = pltpu.roll(mine, HD - turn, 0)
        rows.append(mine)
    return jnp.concatenate(rows, 0).astype(jnp.bfloat16).T


def state_kernel(keys_far, values_far, out_far, keys, values, out, arrived, left):
    loads = [
        pltpu.make_async_copy(keys_far, keys, arrived.at[0]),
        pltpu.make_async_copy(values_far, values, arrived.at[1]),
    ]
    for load in loads:
        load.start()
    stores = []

    def store(strip, begin, end):
        parts = pl.ds(WIDE // TALL * strip, WIDE // TALL)
        lanes = pl.ds(BAND * begin, BAND * (end - begin))
        stores.append(
            pltpu.make_async_copy(out.at[parts, :, lanes], out_far.at[parts, :, lanes], left.at[len(stores)])
        )
        stores[-1].start()

    def put(place, heads):
        strip, place = divmod(place, STRIP)
        for k in range(WIDE // TALL):
            head, row = divmod(k * TALL, HD)
            part = heads[head][row : row + TALL].astype(out.dtype)
            out[WIDE // TALL * strip + k, :, pl.ds(BAND * place, BAND)] = part

    loads[0].wait()
    x = keys[...]
    wide = x.astype(jnp.float32).T
    first = [x, across(wide, False, -1)], [across(wide, True), across(wide, True, -1)]
    loads[1].wait()
    turned_values = values[...].astype(jnp.float32).T.astype(jnp.bfloat16)
    lane = lax.broadcasted_iota(jnp.int32, (1, BAND), 1)
    for s in range(TURNS):
        others = across(wide, False, 0, s) if s else x, across(wide, True, 0, s + TURNS)
        feats = jnp.concatenate([first[swap][k] * others[swap] for k in range(2) for swap in range(2)], 1)
        product = jnp.dot(turned_values, feats, preferred_element_type=jnp.float32)
        for k in range(2):
            plain, swapped = (product[:, BAND * j : BAND * j + BAND] for j in (2 * k, 2 * k + 1))
            heads = [
                jnp.where(lane < HD, plain[:HD], swapped[:HD]),
                jnp.where(lane < HD, swapped[HD:], plain[HD:]),
            ]
            for head in range(HEADS):
                once = (lane < HD) == (head == 0) if s == 0 and k == 0 else lane < 0
                heads[head] = heads[head] * jnp.where(once, 1.0, 2.0)
            put(2 * s + k, heads)
        if 2 * s + 2 == STRIP + 1:
            store(0, 0, STRIP)
        if s == TURNS - 2:
            store(1, 0, 2 * s + 2 - STRIP)
    feats = jnp.concatenate([first[swap][0] * across(wide, swap == 1, 2) for swap in range(2)], 1)
    product = jnp.dot(turned_values, feats, preferred_element_type=jnp.float32)
    heads = []
    for head in range(HEADS):
        mine = product[HD * head : HD * head + HD, BAND * head : BAND * head + BAND]
        heads.append(jnp.where(lane < HD, mine, 0.0))
    put(2 * TURNS, heads)
    put(2 * TURNS + 1, [jnp.zeros((HD, BAND), jnp.float32)] * HEADS)
    store(1, 2 * TURNS - 2 - STRIP, STRIP)
    for copy in stores:
        copy.wait()


def query_band(flat, plain, head, s, lanes):
    rows = pl.ds(head * HD, HD)
    x = plain[rows, lanes]
    blocks = [plain[pl.ds(head * HD + k * BLOCK, BLOCK), lanes] for k in range(BLOCKS)]
    if s == TURNS:
        return x * jnp.concatenate(blocks[2:] + blocks[:2], 0)
    lifted = jnp.concatenate(blocks[-1:] + blocks[:-1], 0)
    turns = (s, s + TURNS) if head == 0 else (s + TURNS, s)
    others = [pltpu.roll(flat[rows, lanes], HD - t, 0).astype(jnp.bfloat16) if t else x for t in turns]
    return jnp.concatenate([first * other for first in (x, lifted) for other in others], 0)


def read_kernel(scale, queries, state, out_far, out, flat, plain, feats, whole, sent):
    for k in range(PARTS):
        strip, rows = divmod(k, WIDE // TALL)
        whole[pl.ds(TALL * rows, TALL), pl.ds(STRIP * BAND * strip, STRIP * BAND)] = state[k].astype(jnp.float32)
    wide = queries[...].astype(jnp.float32).T
    flat[...] = wide
    plain[...] = wide.astype(jnp.bfloat16)
    tokens = queries.shape[0]
    products, stores = [], []
    for head in range(HEADS):
        count = 1 if head == 0 else READS
        size = tokens // count
        for k in range(count):
            lanes = pl.ds(k * size, size)
            product = jnp.zeros((HD, size), jnp.float32)
            begin = 0
            for s in range(TURNS + 1):
                value = query_band(flat, plain, head, s, lanes)
                end = 2 * s * BAND + value.shape[0]
                feats[head, pl.ds(2 * s * BAND, value.shape[0]), lanes] = value
                if s != TURNS - 1:
                    here = whole[pl.ds(head * HD, HD), :][:, begin:end].astype(jnp.bfloat16)
                    right = feats[head, pl.ds(begin, end - begin), lanes]
                    product += jnp.dot(here, right, preferred_element_type=jnp.float32)
                    begin = end
            if head == 0:
                products.append(product)
                continue
            both = jnp.concatenate([products[0][:, k * size : k * size + size], product], 0) * scale[0]
            out[lanes, :] = both.T.astype(out.dtype)
            stores.append(pltpu.make_async_copy(out.at[lanes], out_far.at[lanes], sent.at[k]))
            stores[-1].start()
    for store in stores:
        store.wait()


def in_vmem():
    return pl.BlockSpec(memory_space=pltpu.VMEM)


def in_hbm():
    return pl.BlockSpec(memory_space=pltpu.HBM)


def make_state(keys, values):
    tokens = keys.shape[0]
    part = (TALL, STRIP * BAND)
    return pl.pallas_call(
        state_kernel,
        out_shape=jax.ShapeDtypeStruct((PARTS, *part), jnp.bfloat16),
        in_specs=[in_hbm(), in_hbm()],
        out_specs=in_hbm(),
        scratch_shapes=[
            pltpu.VMEM((tokens, WIDE), jnp.bfloat16),
            pltpu.VMEM((tokens, WIDE), jnp.bfloat16),
            pltpu.VMEM((PARTS, *part), jnp.bfloat16),
            pltpu.SemaphoreType.DMA((2,)),
            pltpu.SemaphoreType.DMA((3,)),
        ],
        compiler_params=pltpu.CompilerParams(vmem_limit_bytes=62 * 2**20),
        name="state",
    )(keys, values)


def read_state(scale, queries, state):
    tokens = queries.shape[0]
    return pl.pallas_call(
        read_kernel,
        out_shape=jax.ShapeDtypeStruct((tokens, WIDE), jnp.bfloat16),
        in_specs=[pl.BlockSpec(memory_space=pltpu.SMEM), in_vmem(), in_vmem()],
        out_specs=in_hbm(),
        scratch_shapes=[
            pltpu.VMEM((tokens, WIDE), jnp.bfloat16),
            pltpu.VMEM((WIDE, tokens), jnp.float32),
            pltpu.VMEM((WIDE, tokens), jnp.bfloat16),
            pltpu.VMEM((HEADS, ROWS, tokens), jnp.bfloat16),
            pltpu.VMEM((WIDE, 2 * STRIP * BAND), jnp.float32),
            pltpu.SemaphoreType.DMA((READS,)),
        ],
        compiler_params=pltpu.CompilerParams(vmem_limit_bytes=48 * 2**20),
        name="read",
    )(scale, queries, state)


def on_device(queries, keys, values):
    plane = lax.axis_size(PLANE)
    groups = lax.axis_size(("pair", "core"))
    shards = plane // groups
    layers = lax.axis_size(DEPTH)
    count = (lax.axis_index(DEPTH + ("pair", "core")) + 1).astype(jnp.float32)
    scale = (1.0 / (HD * jnp.sqrt(count * (queries.shape[0] * shards)))).reshape(1)
    order, place = 0, lax.iota(jnp.int32, layers)
    for axis in DEPTH:
        size = lax.axis_size(axis)
        order, place = order * size + place % size, place // size
    earlier = (order < lax.axis_index(DEPTH)).astype(jnp.float32)
    local = make_state(keys, values)
    part = local.shape[1:]
    local, earlier, scale = lax.optimization_barrier((local, earlier, scale))
    arrived = lax.all_to_all(local, PLANE, 0, 0, tiled=True)
    totals = jnp.sum(arrived.reshape(groups, shards, *part).astype(jnp.float32), 1)
    whole = jnp.sum(totals, 0).astype(jnp.bfloat16)
    copies = jnp.broadcast_to(whole[None], (layers, *part))
    copies, totals, earlier, scale = lax.optimization_barrier((copies, totals, earlier, scale))
    others = lax.all_to_all(copies, DEPTH[::-1], 0, 0, tiled=True)
    before = jnp.sum(others.astype(jnp.float32) * earlier[:, None, None], 0)
    running = []
    for group in range(groups):
        before = before + totals[group]
        running.append(before.astype(jnp.bfloat16))
    inclusive = jnp.stack(running)
    copies = jnp.broadcast_to(inclusive[:, None], (groups, shards, *part))
    copies, scale = lax.optimization_barrier((copies.reshape(plane, *part), scale))
    state = lax.all_to_all(copies, PLANE, 0, 0, tiled=True)
    state, scale = lax.optimization_barrier((state, scale))
    return read_state(scale, queries, state)


def solution(mesh):
    torus = Mesh(mesh.devices.reshape(2, 2, 2, 2, 2, 2, 4), EVERY)
    spec = P(EVERY, None)
    return jax.shard_map(
        on_device, mesh=torus, in_specs=(spec, spec, spec), out_specs=spec, check_vma=False
    )
```

```python
import jax
import jax.numpy as jnp
from jax import lax
from jax.experimental import pallas as pl
from jax.experimental.pallas import tpu as pltpu
from jax.sharding import Mesh
from jax.sharding import PartitionSpec as P

HD = 64
HEADS = 2
WIDE = HEADS * HD
BLOCK = 16
BLOCKS = HD // BLOCK
TURNS = BLOCK // 2
BAND = 2 * HD
ROWS = 2 * TURNS * BAND + HD
STRIP = 9
TALL = 8
READS = 2
PARTS = 2 * WIDE // TALL

DEPTH = ("depth_0", "depth_1", "depth_2")
PLANE = ("pair", "core", "near", "row")
EVERY = DEPTH + PLANE


def across(wide, swap, move=0, turn=0):
    rows = []
    for head in (1, 0) if swap else (0, 1):
        mine = wide[HD * head : HD * head + HD]
        if move:
            mine = jnp.concatenate([mine[BLOCK * (move % BLOCKS) :], mine[: BLOCK * (move % BLOCKS)]], 0)
        if turn:
            mine = pltpu.roll(mine, HD - turn, 0)
        rows.append(mine)
    return jnp.concatenate(rows, 0).astype(jnp.bfloat16).T


def state_kernel(keys_far, values_far, out_far, keys, values, out, arrived, left):
    loads = [
        pltpu.make_async_copy(keys_far, keys, arrived.at[0]),
        pltpu.make_async_copy(values_far, values, arrived.at[1]),
    ]
    for load in loads:
        load.start()
    stores = []

    def store(strip, begin, end):
        parts = pl.ds(WIDE // TALL * strip, WIDE // TALL)
        lanes = pl.ds(BAND * begin, BAND * (end - begin))
        stores.append(
            pltpu.make_async_copy(out.at[parts, :, lanes], out_far.at[parts, :, lanes], left.at[len(stores)])
        )
        stores[-1].start()

    def put(place, heads):
        strip, place = divmod(place, STRIP)
        for k in range(WIDE // TALL):
            head, row = divmod(k * TALL, HD)
            part = heads[head][row : row + TALL].astype(out.dtype)
            out[WIDE // TALL * strip + k, :, pl.ds(BAND * place, BAND)] = part

    loads[0].wait()
    x = keys[...]
    wide = x.astype(jnp.float32).T
    first = [x, across(wide, False, -1)], [across(wide, True), across(wide, True, -1)]
    loads[1].wait()
    turned_values = values[...].astype(jnp.float32).T.astype(jnp.bfloat16)
    lane = lax.broadcasted_iota(jnp.int32, (1, BAND), 1)
    for s in range(TURNS):
        others = across(wide, False, 0, s) if s else x, across(wide, True, 0, s + TURNS)
        feats = jnp.concatenate([first[swap][k] * others[swap] for k in range(2) for swap in range(2)], 1)
        product = jnp.dot(turned_values, feats, preferred_element_type=jnp.float32)
        for k in range(2):
            plain, swapped = (product[:, BAND * j : BAND * j + BAND] for j in (2 * k, 2 * k + 1))
            heads = [
                jnp.where(lane < HD, plain[:HD], swapped[:HD]),
                jnp.where(lane < HD, swapped[HD:], plain[HD:]),
            ]
            for head in range(HEADS):
                once = (lane < HD) == (head == 0) if s == 0 and k == 0 else lane < 0
                heads[head] = heads[head] * jnp.where(once, 1.0, 2.0)
            put(2 * s + k, heads)
        if 2 * s + 2 == STRIP + 1:
            store(0, 0, STRIP)
        if s == TURNS - 2:
            store(1, 0, 2 * s + 2 - STRIP)
    feats = jnp.concatenate([first[swap][0] * across(wide, swap == 1, 2) for swap in range(2)], 1)
    product = jnp.dot(turned_values, feats, preferred_element_type=jnp.float32)
    heads = []
    for head in range(HEADS):
        mine = product[HD * head : HD * head + HD, BAND * head : BAND * head + BAND]
        heads.append(jnp.where(lane < HD, mine, 0.0))
    put(2 * TURNS, heads)
    put(2 * TURNS + 1, [jnp.zeros((HD, BAND), jnp.float32)] * HEADS)
    store(1, 2 * TURNS - 2 - STRIP, STRIP)
    for copy in stores:
        copy.wait()


def query_band(flat, plain, head, s, lanes):
    rows = pl.ds(head * HD, HD)
    x = plain[rows, lanes]
    blocks = [plain[pl.ds(head * HD + k * BLOCK, BLOCK), lanes] for k in range(BLOCKS)]
    if s == TURNS:
        return x * jnp.concatenate(blocks[2:] + blocks[:2], 0)
    lifted = jnp.concatenate(blocks[-1:] + blocks[:-1], 0)
    turns = (s, s + TURNS) if head == 0 else (s + TURNS, s)
    others = [pltpu.roll(flat[rows, lanes], HD - t, 0).astype(jnp.bfloat16) if t else x for t in turns]
    return jnp.concatenate([first * other for first in (x, lifted) for other in others], 0)


def read_kernel(queries, state, out_far, out, flat, plain, feats, whole, sent):
    for k in range(PARTS):
        strip, rows = divmod(k, WIDE // TALL)
        whole[pl.ds(TALL * rows, TALL), pl.ds(STRIP * BAND * strip, STRIP * BAND)] = state[k].astype(jnp.float32)
    wide = queries[...].astype(jnp.float32).T
    flat[...] = wide
    plain[...] = wide.astype(jnp.bfloat16)
    tokens = queries.shape[0]
    products, stores = [], []
    for head in range(HEADS):
        count = 1 if head == 0 else READS
        size = tokens // count
        for k in range(count):
            lanes = pl.ds(k * size, size)
            product = jnp.zeros((HD, size), jnp.float32)
            begin = 0
            for s in range(TURNS + 1):
                value = query_band(flat, plain, head, s, lanes)
                end = 2 * s * BAND + value.shape[0]
                feats[head, pl.ds(2 * s * BAND, value.shape[0]), lanes] = value
                if s != TURNS - 1:
                    here = whole[pl.ds(head * HD, HD), :][:, begin:end].astype(jnp.bfloat16)
                    right = feats[head, pl.ds(begin, end - begin), lanes]
                    product += jnp.dot(here, right, preferred_element_type=jnp.float32)
                    begin = end
            if head == 0:
                products.append(product)
                continue
            both = jnp.concatenate([products[0][:, k * size : k * size + size], product], 0)
            out[lanes, :] = both.T.astype(out.dtype)
            stores.append(pltpu.make_async_copy(out.at[lanes], out_far.at[lanes], sent.at[k]))
            stores[-1].start()
    for store in stores:
        store.wait()


def in_vmem():
    return pl.BlockSpec(memory_space=pltpu.VMEM)


def in_hbm():
    return pl.BlockSpec(memory_space=pltpu.HBM)


def make_state(keys, values):
    tokens = keys.shape[0]
    part = (TALL, STRIP * BAND)
    return pl.pallas_call(
        state_kernel,
        out_shape=jax.ShapeDtypeStruct((PARTS, *part), jnp.bfloat16),
        in_specs=[in_hbm(), in_hbm()],
        out_specs=in_hbm(),
        scratch_shapes=[
            pltpu.VMEM((tokens, WIDE), jnp.bfloat16),
            pltpu.VMEM((tokens, WIDE), jnp.bfloat16),
            pltpu.VMEM((PARTS, *part), jnp.bfloat16),
            pltpu.SemaphoreType.DMA((2,)),
            pltpu.SemaphoreType.DMA((3,)),
        ],
        compiler_params=pltpu.CompilerParams(vmem_limit_bytes=62 * 2**20),
        name="state",
    )(keys, values)


def read_state(queries, state):
    tokens = queries.shape[0]
    return pl.pallas_call(
        read_kernel,
        out_shape=jax.ShapeDtypeStruct((tokens, WIDE), jnp.bfloat16),
        in_specs=[in_vmem(), in_vmem()],
        out_specs=in_hbm(),
        scratch_shapes=[
            pltpu.VMEM((tokens, WIDE), jnp.bfloat16),
            pltpu.VMEM((WIDE, tokens), jnp.float32),
            pltpu.VMEM((WIDE, tokens), jnp.bfloat16),
            pltpu.VMEM((HEADS, ROWS, tokens), jnp.bfloat16),
            pltpu.VMEM((WIDE, 2 * STRIP * BAND), jnp.float32),
            pltpu.SemaphoreType.DMA((READS,)),
        ],
        compiler_params=pltpu.CompilerParams(vmem_limit_bytes=48 * 2**20),
        name="read",
    )(queries, state)


def on_device(queries, keys, values):
    plane = lax.axis_size(PLANE)
    groups = lax.axis_size(("pair", "core"))
    shards = plane // groups
    layers = lax.axis_size(DEPTH)
    first = lax.axis_index(DEPTH) * groups + 1
    tokens = queries.shape[0] * shards
    scale = [1.0 / (HD * jnp.sqrt((first + k).astype(jnp.float32) * tokens)) for k in range(groups)]
    order, place = 0, lax.iota(jnp.int32, layers)
    for axis in DEPTH:
        size = lax.axis_size(axis)
        order, place = order * size + place % size, place // size
    earlier = (order < lax.axis_index(DEPTH)).astype(jnp.float32)
    local = make_state(keys, values)
    part = local.shape[1:]
    local, earlier, scale = lax.optimization_barrier((local, earlier, scale))
    arrived = lax.all_to_all(local, PLANE, 0, 0, tiled=True)
    totals = jnp.sum(arrived.reshape(groups, shards, *part).astype(jnp.float32), 1)
    whole = jnp.sum(totals, 0).astype(jnp.bfloat16)
    copies = jnp.broadcast_to(whole[None], (layers, *part))
    copies, totals, earlier, scale = lax.optimization_barrier((copies, totals, earlier, scale))
    others = lax.all_to_all(copies, DEPTH[::-1], 0, 0, tiled=True)
    before = jnp.sum(others.astype(jnp.float32) * earlier[:, None, None], 0)
    running = []
    for group in range(groups):
        before = before + totals[group]
        running.append((before * scale[group]).astype(jnp.bfloat16))
    inclusive = jnp.stack(running)
    copies = jnp.broadcast_to(inclusive[:, None], (groups, shards, *part))
    state = lax.all_to_all(copies.reshape(plane, *part), PLANE, 0, 0, tiled=True)
    return read_state(queries, state)


def solution(mesh):
    torus = Mesh(mesh.devices.reshape(2, 2, 2, 2, 2, 2, 4), EVERY)
    spec = P(EVERY, None)
    return jax.shard_map(
        on_device, mesh=torus, in_specs=(spec, spec, spec), out_specs=spec, check_vma=False
    )
```

```python
import jax
import jax.numpy as jnp
from jax import lax
from jax.experimental import pallas as pl
from jax.experimental.pallas import tpu as pltpu
from jax.sharding import Mesh
from jax.sharding import PartitionSpec as P

HD = 64
HEADS = 2
WIDE = HEADS * HD
BLOCK = 16
BLOCKS = HD // BLOCK
TURNS = BLOCK // 2
BAND = 2 * HD
ROWS = 2 * TURNS * BAND + HD
STRIP = 9
TALL = 8
READS = 2
PARTS = 2 * WIDE // TALL

DEPTH = ("depth_0", "depth_1", "depth_2")
PLANE = ("pair", "core", "near", "row")
EVERY = DEPTH + PLANE


def across(wide, swap, move=0, turn=0):
    rows = []
    for head in (1, 0) if swap else (0, 1):
        mine = wide[HD * head : HD * head + HD]
        if move:
            mine = jnp.concatenate([mine[BLOCK * (move % BLOCKS) :], mine[: BLOCK * (move % BLOCKS)]], 0)
        if turn:
            mine = pltpu.roll(mine, HD - turn, 0)
        rows.append(mine)
    return jnp.concatenate(rows, 0).astype(jnp.bfloat16).T


def state_kernel(keys_far, values_far, out_far, keys, values, out, arrived, left):
    loads = [
        pltpu.make_async_copy(values_far, values, arrived.at[0]),
        pltpu.make_async_copy(keys_far, keys, arrived.at[1]),
    ]
    for load in loads:
        load.start()
    stores = []

    def store(strip, begin, end):
        parts = pl.ds(WIDE // TALL * strip, WIDE // TALL)
        lanes = pl.ds(BAND * begin, BAND * (end - begin))
        stores.append(
            pltpu.make_async_copy(out.at[parts, :, lanes], out_far.at[parts, :, lanes], left.at[len(stores)])
        )
        stores[-1].start()

    def put(place, heads):
        strip, place = divmod(place, STRIP)
        for k in range(WIDE // TALL):
            head, row = divmod(k * TALL, HD)
            part = heads[head][row : row + TALL].astype(out.dtype)
            out[WIDE // TALL * strip + k, :, pl.ds(BAND * place, BAND)] = part

    loads[0].wait()
    turned_values = values[...].astype(jnp.float32).T.astype(jnp.bfloat16)
    loads[1].wait()
    x = keys[...]
    wide = x.astype(jnp.float32).T
    first = [x, across(wide, False, -1)], [across(wide, True), across(wide, True, -1)]
    lane = lax.broadcasted_iota(jnp.int32, (1, BAND), 1)
    def half_band():
        feats = jnp.concatenate([first[swap][0] * across(wide, swap == 1, 2) for swap in range(2)], 1)
        product = jnp.dot(turned_values, feats, preferred_element_type=jnp.float32)
        heads = []
        for head in range(HEADS):
            mine = product[HD * head : HD * head + HD, BAND * head : BAND * head + BAND]
            heads.append(jnp.where(lane < HD, mine, 0.0))
        put(2 * TURNS, heads)

    put(2 * TURNS + 1, [jnp.zeros((HD, BAND), jnp.float32)] * HEADS)
    half_band()
    store(1, 2 * TURNS - STRIP, STRIP)
    for s in range(TURNS):
        others = across(wide, False, 0, s) if s else x, across(wide, True, 0, s + TURNS)
        feats = jnp.concatenate([first[swap][k] * others[swap] for k in range(2) for swap in range(2)], 1)
        product = jnp.dot(turned_values, feats, preferred_element_type=jnp.float32)
        for k in range(2):
            plain, swapped = (product[:, BAND * j : BAND * j + BAND] for j in (2 * k, 2 * k + 1))
            heads = [
                jnp.where(lane < HD, plain[:HD], swapped[:HD]),
                jnp.where(lane < HD, swapped[HD:], plain[HD:]),
            ]
            for head in range(HEADS):
                once = (lane < HD) == (head == 0) if s == 0 and k == 0 else lane < 0
                heads[head] = heads[head] * jnp.where(once, 1.0, 2.0)
            put(2 * s + k, heads)
        if 2 * s + 2 == STRIP + 1:
            store(0, 0, STRIP)
        if s == TURNS - 2:
            store(1, 0, 2 * s + 2 - STRIP)
    store(1, 2 * TURNS - 2 - STRIP, 2 * TURNS - STRIP)
    for copy in stores:
        copy.wait()


def query_band(flat, plain, head, s, lanes):
    rows = pl.ds(head * HD, HD)
    x = plain[rows, lanes]
    blocks = [plain[pl.ds(head * HD + k * BLOCK, BLOCK), lanes] for k in range(BLOCKS)]
    if s == TURNS:
        return x * jnp.concatenate(blocks[2:] + blocks[:2], 0)
    lifted = jnp.concatenate(blocks[-1:] + blocks[:-1], 0)
    turns = (s, s + TURNS) if head == 0 else (s + TURNS, s)
    others = [pltpu.roll(flat[rows, lanes], HD - t, 0).astype(jnp.bfloat16) if t else x for t in turns]
    return jnp.concatenate([first * other for first in (x, lifted) for other in others], 0)


def read_kernel(scale, queries, state, out_far, out, flat, plain, feats, whole, sent):
    for k in range(PARTS):
        strip, rows = divmod(k, WIDE // TALL)
        whole[pl.ds(TALL * rows, TALL), pl.ds(STRIP * BAND * strip, STRIP * BAND)] = state[k].astype(jnp.float32)
    wide = queries[...].astype(jnp.float32).T
    flat[...] = wide
    plain[...] = wide.astype(jnp.bfloat16)
    tokens = queries.shape[0]
    products, stores = [], []
    for head in range(HEADS):
        count = 1 if head == 0 else READS
        size = tokens // count
        for k in range(count):
            lanes = pl.ds(k * size, size)
            product = jnp.zeros((HD, size), jnp.float32)
            begin = 0
            for s in range(TURNS + 1):
                value = query_band(flat, plain, head, s, lanes)
                end = 2 * s * BAND + value.shape[0]
                feats[head, pl.ds(2 * s * BAND, value.shape[0]), lanes] = value
                if s != TURNS - 1:
                    here = whole[pl.ds(head * HD, HD), :][:, begin:end].astype(jnp.bfloat16)
                    right = feats[head, pl.ds(begin, end - begin), lanes]
                    product += jnp.dot(here, right, preferred_element_type=jnp.float32)
                    begin = end
            if head == 0:
                products.append(product)
                continue
            both = jnp.concatenate([products[0][:, k * size : k * size + size], product], 0) * scale[0]
            out[lanes, :] = both.T.astype(out.dtype)
            stores.append(pltpu.make_async_copy(out.at[lanes], out_far.at[lanes], sent.at[k]))
            stores[-1].start()
    for store in stores:
        store.wait()


def in_vmem():
    return pl.BlockSpec(memory_space=pltpu.VMEM)


def in_hbm():
    return pl.BlockSpec(memory_space=pltpu.HBM)


def make_state(keys, values):
    tokens = keys.shape[0]
    part = (TALL, STRIP * BAND)
    return pl.pallas_call(
        state_kernel,
        out_shape=jax.ShapeDtypeStruct((PARTS, *part), jnp.bfloat16),
        in_specs=[in_hbm(), in_hbm()],
        out_specs=in_hbm(),
        scratch_shapes=[
            pltpu.VMEM((tokens, WIDE), jnp.bfloat16),
            pltpu.VMEM((tokens, WIDE), jnp.bfloat16),
            pltpu.VMEM((PARTS, *part), jnp.bfloat16),
            pltpu.SemaphoreType.DMA((2,)),
            pltpu.SemaphoreType.DMA((4,)),
        ],
        compiler_params=pltpu.CompilerParams(vmem_limit_bytes=62 * 2**20),
        name="state",
    )(keys, values)


def read_state(scale, queries, state):
    tokens = queries.shape[0]
    return pl.pallas_call(
        read_kernel,
        out_shape=jax.ShapeDtypeStruct((tokens, WIDE), jnp.bfloat16),
        in_specs=[pl.BlockSpec(memory_space=pltpu.SMEM), in_vmem(), in_vmem()],
        out_specs=in_hbm(),
        scratch_shapes=[
            pltpu.VMEM((tokens, WIDE), jnp.bfloat16),
            pltpu.VMEM((WIDE, tokens), jnp.float32),
            pltpu.VMEM((WIDE, tokens), jnp.bfloat16),
            pltpu.VMEM((HEADS, ROWS, tokens), jnp.bfloat16),
            pltpu.VMEM((WIDE, 2 * STRIP * BAND), jnp.float32),
            pltpu.SemaphoreType.DMA((READS,)),
        ],
        compiler_params=pltpu.CompilerParams(vmem_limit_bytes=48 * 2**20),
        name="read",
    )(scale, queries, state)


def on_device(queries, keys, values):
    plane = lax.axis_size(PLANE)
    groups = lax.axis_size(("pair", "core"))
    shards = plane // groups
    layers = lax.axis_size(DEPTH)
    count = (lax.axis_index(DEPTH + ("pair", "core")) + 1).astype(jnp.float32)
    scale = (1.0 / (HD * jnp.sqrt(count * (queries.shape[0] * shards)))).reshape(1)
    order, place = 0, lax.iota(jnp.int32, layers)
    for axis in DEPTH:
        size = lax.axis_size(axis)
        order, place = order * size + place % size, place // size
    earlier = (order < lax.axis_index(DEPTH)).astype(jnp.float32)
    local = make_state(keys, values)
    part = local.shape[1:]
    local, earlier, scale = lax.optimization_barrier((local, earlier, scale))
    arrived = lax.all_to_all(local, PLANE, 0, 0, tiled=True)
    totals = jnp.sum(arrived.reshape(groups, shards, *part).astype(jnp.float32), 1)
    whole = jnp.sum(totals, 0).astype(jnp.bfloat16)
    copies = jnp.broadcast_to(whole[None], (layers, *part))
    copies, totals, earlier, scale = lax.optimization_barrier((copies, totals, earlier, scale))
    others = lax.all_to_all(copies, DEPTH[::-1], 0, 0, tiled=True)
    before = jnp.sum(others.astype(jnp.float32) * earlier[:, None, None], 0)
    running = []
    for group in range(groups):
        before = before + totals[group]
        running.append(before.astype(jnp.bfloat16))
    inclusive = jnp.stack(running)
    copies = jnp.broadcast_to(inclusive[:, None], (groups, shards, *part))
    copies, scale = lax.optimization_barrier((copies.reshape(plane, *part), scale))
    state = lax.all_to_all(copies, PLANE, 0, 0, tiled=True)
    state, scale = lax.optimization_barrier((state, scale))
    return read_state(scale, queries, state)


def solution(mesh):
    torus = Mesh(mesh.devices.reshape(2, 2, 2, 2, 2, 2, 4), EVERY)
    spec = P(EVERY, None)
    return jax.shard_map(
        on_device, mesh=torus, in_specs=(spec, spec, spec), out_specs=spec, check_vma=False
    )
```

```python
import jax
import jax.numpy as jnp
from jax import lax
from jax.experimental import pallas as pl
from jax.experimental.pallas import tpu as pltpu
from jax.sharding import Mesh
from jax.sharding import PartitionSpec as P

HD = 64
HEADS = 2
WIDE = HEADS * HD
BLOCK = 16
BLOCKS = HD // BLOCK
TURNS = BLOCK // 2
BAND = 2 * HD
ROWS = 2 * TURNS * BAND + HD
STRIP = 9
TALL = 8
PARTS = 2 * WIDE // TALL

DEPTH = ("depth_0", "depth_1", "depth_2")
PLANE = ("pair", "core", "near", "row")
EVERY = DEPTH + PLANE


def across(wide, swap, move=0, turn=0):
    rows = []
    for head in (1, 0) if swap else (0, 1):
        mine = wide[HD * head : HD * head + HD]
        if move:
            mine = jnp.concatenate([mine[BLOCK * (move % BLOCKS) :], mine[: BLOCK * (move % BLOCKS)]], 0)
        if turn:
            mine = pltpu.roll(mine, HD - turn, 0)
        rows.append(mine)
    return jnp.concatenate(rows, 0).astype(jnp.bfloat16).T


def state_kernel(keys_far, values_far, out_far, keys, values, out, arrived, left):
    loads = [
        pltpu.make_async_copy(values_far, values, arrived.at[0]),
        pltpu.make_async_copy(keys_far, keys, arrived.at[1]),
    ]
    for load in loads:
        load.start()
    stores = []

    def store(strip, begin, end):
        parts = pl.ds(WIDE // TALL * strip, WIDE // TALL)
        lanes = pl.ds(BAND * begin, BAND * (end - begin))
        stores.append(
            pltpu.make_async_copy(out.at[parts, :, lanes], out_far.at[parts, :, lanes], left.at[len(stores)])
        )
        stores[-1].start()

    def put(place, heads):
        strip, place = divmod(place, STRIP)
        for k in range(WIDE // TALL):
            head, row = divmod(k * TALL, HD)
            part = heads[head][row : row + TALL].astype(out.dtype)
            out[WIDE // TALL * strip + k, :, pl.ds(BAND * place, BAND)] = part

    loads[0].wait()
    turned_values = values[...].astype(jnp.float32).T.astype(jnp.bfloat16)
    loads[1].wait()
    x = keys[...]
    wide = x.astype(jnp.float32).T
    first = [x, across(wide, False, -1)], [across(wide, True), across(wide, True, -1)]
    lane = lax.broadcasted_iota(jnp.int32, (1, BAND), 1)

    def half_band():
        feats = jnp.concatenate([first[swap][0] * across(wide, swap == 1, 2) for swap in range(2)], 1)
        product = jnp.dot(turned_values, feats, preferred_element_type=jnp.float32)
        heads = []
        for head in range(HEADS):
            mine = product[HD * head : HD * head + HD, BAND * head : BAND * head + BAND]
            heads.append(jnp.where(lane < HD, mine, 0.0))
        put(2 * TURNS, heads)

    put(2 * TURNS + 1, [jnp.zeros((HD, BAND), jnp.float32)] * HEADS)
    half_band()
    store(1, 2 * TURNS - STRIP, STRIP)
    for s in range(TURNS):
        others = across(wide, False, 0, s) if s else x, across(wide, True, 0, s + TURNS)
        feats = jnp.concatenate([first[swap][k] * others[swap] for k in range(2) for swap in range(2)], 1)
        product = jnp.dot(turned_values, feats, preferred_element_type=jnp.float32)
        for k in range(2):
            plain, swapped = (product[:, BAND * j : BAND * j + BAND] for j in (2 * k, 2 * k + 1))
            heads = [
                jnp.where(lane < HD, plain[:HD], swapped[:HD]),
                jnp.where(lane < HD, swapped[HD:], plain[HD:]),
            ]
            for head in range(HEADS):
                once = (lane < HD) == (head == 0) if s == 0 and k == 0 else lane < 0
                heads[head] = heads[head] * jnp.where(once, 1.0, 2.0)
            put(2 * s + k, heads)
        if 2 * s + 2 == STRIP + 1:
            store(0, 0, STRIP)
        if s == TURNS - 2:
            store(1, 0, 2 * s + 2 - STRIP)
    store(1, 2 * TURNS - 2 - STRIP, 2 * TURNS - STRIP)
    for copy in stores:
        copy.wait()


def query_band(flat, plain, head, s):
    rows = pl.ds(head * HD, HD)
    x = plain[rows, :]
    blocks = [plain[pl.ds(head * HD + k * BLOCK, BLOCK), :] for k in range(BLOCKS)]
    if s == TURNS:
        return x * jnp.concatenate(blocks[2:] + blocks[:2], 0)
    lifted = jnp.concatenate(blocks[-1:] + blocks[:-1], 0)
    turns = (s, s + TURNS) if head == 0 else (s + TURNS, s)
    others = [pltpu.roll(flat[rows, :], HD - t, 0).astype(jnp.bfloat16) if t else x for t in turns]
    return jnp.concatenate([first * other for first in (x, lifted) for other in others], 0)


def read_kernel(scale, queries, state, out_far, out, flat, plain, feats, sent):
    def rows_of(head):
        strips = []
        for strip in range(2):
            first = WIDE // TALL * strip + HD // TALL * head
            strips.append(jnp.concatenate([state[first + k].astype(jnp.float32) for k in range(HD // TALL)], 0))
        return jnp.concatenate(strips, 1).astype(jnp.bfloat16)

    wide = queries[...].astype(jnp.float32).T
    flat[...] = wide
    plain[...] = wide.astype(jnp.bfloat16)
    tokens = queries.shape[0]
    products = []
    for head in range(HEADS):
        mine = rows_of(head)
        product = jnp.zeros((HD, tokens), jnp.float32)
        begin = 0
        for s in range(TURNS + 1):
            value = query_band(flat, plain, head, s)
            end = 2 * s * BAND + value.shape[0]
            feats[head, pl.ds(2 * s * BAND, value.shape[0]), :] = value
            if s != TURNS - 1:
                right = feats[head, pl.ds(begin, end - begin), :]
                product += jnp.dot(mine[:, begin:end], right, preferred_element_type=jnp.float32)
                begin = end
        products.append(product)
    result = jnp.concatenate(products, 0) * scale[0]
    out[...] = result.T.astype(out.dtype)
    store = pltpu.make_async_copy(out, out_far, sent)
    store.start()
    store.wait()


def in_vmem():
    return pl.BlockSpec(memory_space=pltpu.VMEM)


def in_hbm():
    return pl.BlockSpec(memory_space=pltpu.HBM)


def make_state(keys, values):
    tokens = keys.shape[0]
    part = (TALL, STRIP * BAND)
    return pl.pallas_call(
        state_kernel,
        out_shape=jax.ShapeDtypeStruct((PARTS, *part), jnp.bfloat16),
        in_specs=[in_hbm(), in_hbm()],
        out_specs=in_hbm(),
        scratch_shapes=[
            pltpu.VMEM((tokens, WIDE), jnp.bfloat16),
            pltpu.VMEM((tokens, WIDE), jnp.bfloat16),
            pltpu.VMEM((PARTS, *part), jnp.bfloat16),
            pltpu.SemaphoreType.DMA((2,)),
            pltpu.SemaphoreType.DMA((4,)),
        ],
        compiler_params=pltpu.CompilerParams(vmem_limit_bytes=60 * 2**20),
        name="state",
    )(keys, values)


def read_state(scale, queries, state):
    tokens = queries.shape[0]
    return pl.pallas_call(
        read_kernel,
        out_shape=jax.ShapeDtypeStruct((tokens, WIDE), jnp.bfloat16),
        in_specs=[pl.BlockSpec(memory_space=pltpu.SMEM), in_vmem(), in_vmem()],
        out_specs=in_hbm(),
        scratch_shapes=[
            pltpu.VMEM((tokens, WIDE), jnp.bfloat16),
            pltpu.VMEM((WIDE, tokens), jnp.float32),
            pltpu.VMEM((WIDE, tokens), jnp.bfloat16),
            pltpu.VMEM((HEADS, ROWS, tokens), jnp.bfloat16),
            pltpu.SemaphoreType.DMA,
        ],
        compiler_params=pltpu.CompilerParams(vmem_limit_bytes=48 * 2**20),
        name="read",
    )(scale, queries, state)


def on_device(queries, keys, values):
    plane = lax.axis_size(PLANE)
    groups = lax.axis_size(("pair", "core"))
    shards = plane // groups
    layers = lax.axis_size(DEPTH)
    count = (lax.axis_index(DEPTH + ("pair", "core")) + 1).astype(jnp.float32)
    scale = (1.0 / (HD * jnp.sqrt(count * (queries.shape[0] * shards)))).reshape(1)
    order, place = 0, lax.iota(jnp.int32, layers)
    for axis in DEPTH:
        size = lax.axis_size(axis)
        order, place = order * size + place % size, place // size
    earlier = (order < lax.axis_index(DEPTH)).astype(jnp.float32)
    local = make_state(keys, values)
    part = local.shape[1:]
    local, earlier, scale = lax.optimization_barrier((local, earlier, scale))
    arrived = lax.all_to_all(local, PLANE, 0, 0, tiled=True)
    totals = jnp.sum(arrived.reshape(groups, shards, *part).astype(jnp.float32), 1)
    whole = jnp.sum(totals, 0).astype(jnp.bfloat16)
    copies = jnp.broadcast_to(whole[None], (layers, *part))
    copies, totals, earlier, scale = lax.optimization_barrier((copies, totals, earlier, scale))
    others = lax.all_to_all(copies, DEPTH[::-1], 0, 0, tiled=True)
    before = jnp.sum(others.astype(jnp.float32) * earlier[:, None, None], 0)
    running = []
    for group in range(groups):
        before = before + totals[group]
        running.append(before.astype(jnp.bfloat16))
    inclusive = jnp.stack(running)
    copies = jnp.broadcast_to(inclusive[:, None], (groups, shards, *part))
    copies, scale = lax.optimization_barrier((copies.reshape(plane, *part), scale))
    state = lax.all_to_all(copies, PLANE, 0, 0, tiled=True)
    state, scale = lax.optimization_barrier((state, scale))
    return read_state(scale, queries, state)


def solution(mesh):
    torus = Mesh(mesh.devices.reshape(2, 2, 2, 2, 2, 2, 4), EVERY)
    spec = P(EVERY, None)
    return jax.shard_map(
        on_device, mesh=torus, in_specs=(spec, spec, spec), out_specs=spec, check_vma=False
    )
```

```python
import jax
import jax.numpy as jnp
from jax import lax
from jax.experimental import pallas as pl
from jax.experimental.pallas import tpu as pltpu
from jax.sharding import Mesh
from jax.sharding import PartitionSpec as P

HD = 64
HEADS = 2
WIDE = HEADS * HD
BLOCK = 16
BLOCKS = HD // BLOCK
TURNS = BLOCK // 2
BAND = 2 * HD
ROWS = 2 * TURNS * BAND
STRIP = 9
TALL = 8
PARTS = 2 * WIDE // TALL

DEPTH = ("depth_0", "depth_1", "depth_2")
PLANE = ("pair", "core", "near", "row")
EVERY = DEPTH + PLANE


def across(wide, swap, move=0, turn=0):
    rows = []
    for head in (1, 0) if swap else (0, 1):
        mine = wide[HD * head : HD * head + HD]
        if move:
            mine = jnp.concatenate([mine[BLOCK * (move % BLOCKS) :], mine[: BLOCK * (move % BLOCKS)]], 0)
        if turn:
            mine = pltpu.roll(mine, HD - turn, 0)
        rows.append(mine)
    return jnp.concatenate(rows, 0).astype(jnp.bfloat16).T


def state_kernel(keys_far, values_far, out_far, keys, values, out, arrived, left):
    loads = [
        pltpu.make_async_copy(values_far, values, arrived.at[0]),
        pltpu.make_async_copy(keys_far, keys, arrived.at[1]),
    ]
    for load in loads:
        load.start()
    stores = []

    def store(strip, begin, end):
        parts = pl.ds(WIDE // TALL * strip, WIDE // TALL)
        lanes = pl.ds(BAND * begin, BAND * (end - begin))
        stores.append(
            pltpu.make_async_copy(out.at[parts, :, lanes], out_far.at[parts, :, lanes], left.at[len(stores)])
        )
        stores[-1].start()

    def put(place, heads):
        strip, place = divmod(place, STRIP)
        for k in range(WIDE // TALL):
            head, row = divmod(k * TALL, HD)
            part = heads[head][row : row + TALL].astype(out.dtype)
            out[WIDE // TALL * strip + k, :, pl.ds(BAND * place, BAND)] = part

    loads[0].wait()
    turned_values = values[...].astype(jnp.float32).T.astype(jnp.bfloat16)
    loads[1].wait()
    x = keys[...]
    wide = x.astype(jnp.float32).T
    first = [x, across(wide, False, -1)], [across(wide, True), across(wide, True, -1)]
    lane = lax.broadcasted_iota(jnp.int32, (1, BAND), 1)

    product = jnp.dot(turned_values, x * across(wide, False, 2), preferred_element_type=jnp.float32)
    heads = [product[HD * head : HD * head + HD] for head in range(HEADS)]
    put(2 * TURNS, [jnp.where((lane < HD) == (head == 0), heads[head], 0.0) for head in range(HEADS)])
    put(2 * TURNS + 1, [jnp.zeros((HD, BAND), jnp.float32)] * HEADS)
    store(1, 2 * TURNS - STRIP, STRIP)
    for s in range(TURNS):
        others = across(wide, False, 0, s) if s else x, across(wide, True, 0, s + TURNS)
        feats = jnp.concatenate([first[swap][k] * others[swap] for k in range(2) for swap in range(2)], 1)
        product = jnp.dot(turned_values, feats, preferred_element_type=jnp.float32)
        for k in range(2):
            plain, swapped = (product[:, BAND * j : BAND * j + BAND] for j in (2 * k, 2 * k + 1))
            heads = [
                jnp.where(lane < HD, plain[:HD], swapped[:HD]),
                jnp.where(lane < HD, swapped[HD:], plain[HD:]),
            ]
            for head in range(HEADS):
                once = (lane < HD) == (head == 0) if s == 0 and k == 0 else lane < 0
                heads[head] = heads[head] * jnp.where(once, 1.0, 2.0)
            put(2 * s + k, heads)
        if 2 * s + 2 == STRIP + 1:
            store(0, 0, STRIP)
        if s == TURNS - 2:
            store(1, 0, 2 * s + 2 - STRIP)
    store(1, 2 * TURNS - 2 - STRIP, 2 * TURNS - STRIP)
    for copy in stores:
        copy.wait()


def query_band(flat, plain, head, s):
    rows = pl.ds(head * HD, HD)
    x = plain[rows, :]
    blocks = [plain[pl.ds(head * HD + k * BLOCK, BLOCK), :] for k in range(BLOCKS)]
    if s == TURNS:
        return x * jnp.concatenate(blocks[2:] + blocks[:2], 0)
    lifted = jnp.concatenate(blocks[-1:] + blocks[:-1], 0)
    turns = (s, s + TURNS) if head == 0 else (s + TURNS, s)
    others = [pltpu.roll(flat[rows, :], HD - t, 0).astype(jnp.bfloat16) if t else x for t in turns]
    return jnp.concatenate([first * other for first in (x, lifted) for other in others], 0)


def read_kernel(scale, queries, state, out_far, out, flat, plain, feats, sent):
    def rows_of(head):
        strips = []
        for strip in range(2):
            first = WIDE // TALL * strip + HD // TALL * head
            strips.append(jnp.concatenate([state[first + k].astype(jnp.float32) for k in range(HD // TALL)], 0))
        return jnp.concatenate(strips, 1).astype(jnp.bfloat16)

    wide = queries[...].astype(jnp.float32).T
    flat[...] = wide
    plain[...] = wide.astype(jnp.bfloat16)
    mine = [rows_of(head) for head in range(HEADS)]
    halves = [query_band(flat, plain, head, TURNS) for head in range(HEADS)]
    last = jnp.concatenate([rows[:, 2 * TURNS * BAND : 2 * TURNS * BAND + BAND] for rows in mine], 0)
    ends = jnp.dot(last, jnp.concatenate(halves, 0), preferred_element_type=jnp.float32)
    products = []
    for head in range(HEADS):
        product = ends[HD * head : HD * head + HD]
        for s in range(TURNS):
            here = pl.ds(2 * s * BAND, 2 * BAND)
            feats[head, here, :] = query_band(flat, plain, head, s)
            left = mine[head][:, 2 * s * BAND : 2 * s * BAND + 2 * BAND]
            product += jnp.dot(left, feats[head, here, :], preferred_element_type=jnp.float32)
        products.append(product)
    result = jnp.concatenate(products, 0) * scale[0]
    out[...] = result.T.astype(out.dtype)
    store = pltpu.make_async_copy(out, out_far, sent)
    store.start()
    store.wait()


def in_vmem():
    return pl.BlockSpec(memory_space=pltpu.VMEM)


def in_hbm():
    return pl.BlockSpec(memory_space=pltpu.HBM)


def make_state(keys, values):
    tokens = keys.shape[0]
    part = (TALL, STRIP * BAND)
    return pl.pallas_call(
        state_kernel,
        out_shape=jax.ShapeDtypeStruct((PARTS, *part), jnp.bfloat16),
        in_specs=[in_hbm(), in_hbm()],
        out_specs=in_hbm(),
        scratch_shapes=[
            pltpu.VMEM((tokens, WIDE), jnp.bfloat16),
            pltpu.VMEM((tokens, WIDE), jnp.bfloat16),
            pltpu.VMEM((PARTS, *part), jnp.bfloat16),
            pltpu.SemaphoreType.DMA((2,)),
            pltpu.SemaphoreType.DMA((4,)),
        ],
        compiler_params=pltpu.CompilerParams(vmem_limit_bytes=60 * 2**20),
        name="state",
    )(keys, values)


def read_state(scale, queries, state):
    tokens = queries.shape[0]
    return pl.pallas_call(
        read_kernel,
        out_shape=jax.ShapeDtypeStruct((tokens, WIDE), jnp.bfloat16),
        in_specs=[pl.BlockSpec(memory_space=pltpu.SMEM), in_vmem(), in_vmem()],
        out_specs=in_hbm(),
        scratch_shapes=[
            pltpu.VMEM((tokens, WIDE), jnp.bfloat16),
            pltpu.VMEM((WIDE, tokens), jnp.float32),
            pltpu.VMEM((WIDE, tokens), jnp.bfloat16),
            pltpu.VMEM((HEADS, ROWS, tokens), jnp.bfloat16),
            pltpu.SemaphoreType.DMA,
        ],
        compiler_params=pltpu.CompilerParams(vmem_limit_bytes=48 * 2**20),
        name="read",
    )(scale, queries, state)


def on_device(queries, keys, values):
    plane = lax.axis_size(PLANE)
    groups = lax.axis_size(("pair", "core"))
    shards = plane // groups
    layers = lax.axis_size(DEPTH)
    count = (lax.axis_index(DEPTH + ("pair", "core")) + 1).astype(jnp.float32)
    scale = (1.0 / (HD * jnp.sqrt(count * (queries.shape[0] * shards)))).reshape(1)
    order, place = 0, lax.iota(jnp.int32, layers)
    for axis in DEPTH:
        size = lax.axis_size(axis)
        order, place = order * size + place % size, place // size
    earlier = (order < lax.axis_index(DEPTH)).astype(jnp.float32)
    local = make_state(keys, values)
    part = local.shape[1:]
    local, earlier, scale = lax.optimization_barrier((local, earlier, scale))
    arrived = lax.all_to_all(local, PLANE, 0, 0, tiled=True)
    totals = jnp.sum(arrived.reshape(groups, shards, *part).astype(jnp.float32), 1)
    whole = jnp.sum(totals, 0).astype(jnp.bfloat16)
    copies = jnp.broadcast_to(whole[None], (layers, *part))
    copies, totals, earlier, scale = lax.optimization_barrier((copies, totals, earlier, scale))
    others = lax.all_to_all(copies, DEPTH[::-1], 0, 0, tiled=True)
    before = jnp.sum(others.astype(jnp.float32) * earlier[:, None, None], 0)
    running = []
    for group in range(groups):
        before = before + totals[group]
        running.append(before.astype(jnp.bfloat16))
    inclusive = jnp.stack(running)
    copies = jnp.broadcast_to(inclusive[:, None], (groups, shards, *part))
    copies, scale = lax.optimization_barrier((copies.reshape(plane, *part), scale))
    state = lax.all_to_all(copies, PLANE, 0, 0, tiled=True)
    state, scale = lax.optimization_barrier((state, scale))
    return read_state(scale, queries, state)


def solution(mesh):
    torus = Mesh(mesh.devices.reshape(2, 2, 2, 2, 2, 2, 4), EVERY)
    spec = P(EVERY, None)
    return jax.shard_map(
        on_device, mesh=torus, in_specs=(spec, spec, spec), out_specs=spec, check_vma=False
    )
```

```python
import jax
import jax.numpy as jnp
from jax import lax
from jax.experimental import pallas as pl
from jax.experimental.pallas import tpu as pltpu
from jax.sharding import Mesh
from jax.sharding import PartitionSpec as P

HD = 64
HEADS = 2
WIDE = HEADS * HD
BLOCK = 16
BLOCKS = HD // BLOCK
TURNS = BLOCK // 2
BAND = 2 * HD
ROWS = 2 * TURNS * BAND
STRIP = 9
TALL = 8
TILE = 2048
PARTS = 2 * WIDE // TALL

DEPTH = ("depth_0", "depth_1", "depth_2")
PLANE = ("pair", "core", "near", "row")
EVERY = DEPTH + PLANE


def across(wide, swap, move=0, turn=0):
    rows = []
    for head in (1, 0) if swap else (0, 1):
        mine = wide[HD * head : HD * head + HD]
        if move:
            mine = jnp.concatenate([mine[BLOCK * (move % BLOCKS) :], mine[: BLOCK * (move % BLOCKS)]], 0)
        if turn:
            mine = pltpu.roll(mine, HD - turn, 0)
        rows.append(mine)
    return jnp.concatenate(rows, 0).astype(jnp.bfloat16).T


def state_kernel(keys_far, values_far, out_far, keys, values, out, arrived, left):
    loads = [
        pltpu.make_async_copy(values_far, values, arrived.at[0]),
        pltpu.make_async_copy(keys_far, keys, arrived.at[1]),
    ]
    for load in loads:
        load.start()
    stores = []

    def store(strip, begin, end):
        parts = pl.ds(WIDE // TALL * strip, WIDE // TALL)
        lanes = pl.ds(BAND * begin, BAND * (end - begin))
        stores.append(
            pltpu.make_async_copy(out.at[parts, :, lanes], out_far.at[parts, :, lanes], left.at[len(stores)])
        )
        stores[-1].start()

    def put(place, heads):
        strip, place = divmod(place, STRIP)
        for k in range(WIDE // TALL):
            head, row = divmod(k * TALL, HD)
            part = heads[head][row : row + TALL].astype(out.dtype)
            out[WIDE // TALL * strip + k, :, pl.ds(BAND * place, BAND)] = part

    loads[0].wait()
    turned_values = values[...].astype(jnp.float32).T.astype(jnp.bfloat16)
    loads[1].wait()
    x = keys[...]
    wide = x.astype(jnp.float32).T
    first = [x, across(wide, False, -1)], [across(wide, True), across(wide, True, -1)]
    lane = lax.broadcasted_iota(jnp.int32, (1, BAND), 1)

    product = jnp.dot(turned_values, x * across(wide, False, 2), preferred_element_type=jnp.float32)
    heads = [product[HD * head : HD * head + HD] for head in range(HEADS)]
    put(2 * TURNS, [jnp.where((lane < HD) == (head == 0), heads[head], 0.0) for head in range(HEADS)])
    put(2 * TURNS + 1, [jnp.zeros((HD, BAND), jnp.float32)] * HEADS)
    store(1, 2 * TURNS - STRIP, STRIP)
    for s in range(TURNS):
        others = across(wide, False, 0, s) if s else x, across(wide, True, 0, s + TURNS)
        feats = jnp.concatenate([first[swap][k] * others[swap] for k in range(2) for swap in range(2)], 1)
        product = jnp.dot(turned_values, feats, preferred_element_type=jnp.float32)
        for k in range(2):
            plain, swapped = (product[:, BAND * j : BAND * j + BAND] for j in (2 * k, 2 * k + 1))
            heads = [
                jnp.where(lane < HD, plain[:HD], swapped[:HD]),
                jnp.where(lane < HD, swapped[HD:], plain[HD:]),
            ]
            for head in range(HEADS):
                once = (lane < HD) == (head == 0) if s == 0 and k == 0 else lane < 0
                heads[head] = heads[head] * jnp.where(once, 1.0, 2.0)
            put(2 * s + k, heads)
        if 2 * s + 2 == STRIP + 1:
            store(0, 0, STRIP)
        if s == TURNS - 2:
            store(1, 0, 2 * s + 2 - STRIP)
    store(1, 2 * TURNS - 2 - STRIP, 2 * TURNS - STRIP)
    for copy in stores:
        copy.wait()


def query_band(wide, x, s):
    blocks = [x[k * BLOCK : k * BLOCK + BLOCK] for k in range(BLOCKS)]
    if s == TURNS:
        return x * jnp.concatenate(blocks[2:] + blocks[:2], 0)
    lifted = jnp.concatenate(blocks[-1:] + blocks[:-1], 0)
    others = [pltpu.roll(wide, HD - t, 0).astype(jnp.bfloat16) if t else x for t in (s, s + TURNS)]
    return [first * other for first in (x, lifted) for other in others]


def read_kernel(scale, queries, state, out_far, out, feats, whole, sent):
    for head in range(HEADS):
        for strip in range(2):
            first = WIDE // TALL * strip + HD // TALL * head
            rows = jnp.concatenate([state[first + k].astype(jnp.float32) for k in range(HD // TALL)], 0)
            whole[pl.ds(HD * head, HD), pl.ds(STRIP * BAND * strip, STRIP * BAND)] = rows.astype(jnp.bfloat16)

    def store(step):
        rows = pl.ds(pl.multiple_of(step * TILE, TILE), TILE)
        return pltpu.make_async_copy(out.at[rows], out_far.at[rows], sent.at[step])

    @pl.loop(0, out.shape[0] // TILE)
    def _(step):
        rows = pl.ds(pl.multiple_of(step * TILE, TILE), TILE)
        wide = queries[rows, :].astype(jnp.float32).T
        plain = wide.astype(jnp.bfloat16)
        heads = [pl.ds(HD * head, HD) for head in range(HEADS)]
        halves = [query_band(None, plain[HD * head : HD * head + HD], TURNS) for head in range(HEADS)]
        last = whole[:, pl.ds(2 * TURNS * BAND, BAND)]
        ends = jnp.dot(last, jnp.concatenate(halves, 0), preferred_element_type=jnp.float32)
        products = []
        for head in range(HEADS):
            here = slice(HD * head, HD * head + HD)
            for s in range(TURNS):
                parts = query_band(wide[here], plain[here], s)
                if head == 1:
                    parts = [parts[k] for k in (1, 0, 3, 2)]
                feats[head, pl.ds(2 * s * BAND, 2 * BAND), :] = jnp.concatenate(parts, 0)
            left = whole[heads[head], pl.ds(0, ROWS)]
            product = jnp.dot(left, feats[head], preferred_element_type=jnp.float32)
            products.append(ends[here] + product)
        result = jnp.concatenate(products, 0) * scale[0]
        out[rows, :] = result.T.astype(out.dtype)
        store(step).start()

    for step in range(out.shape[0] // TILE):
        store(step).wait()


def in_vmem():
    return pl.BlockSpec(memory_space=pltpu.VMEM)


def in_hbm():
    return pl.BlockSpec(memory_space=pltpu.HBM)


def make_state(keys, values):
    tokens = keys.shape[0]
    part = (TALL, STRIP * BAND)
    return pl.pallas_call(
        state_kernel,
        out_shape=jax.ShapeDtypeStruct((PARTS, *part), jnp.bfloat16),
        in_specs=[in_hbm(), in_hbm()],
        out_specs=in_hbm(),
        scratch_shapes=[
            pltpu.VMEM((tokens, WIDE), jnp.bfloat16),
            pltpu.VMEM((tokens, WIDE), jnp.bfloat16),
            pltpu.VMEM((PARTS, *part), jnp.bfloat16),
            pltpu.SemaphoreType.DMA((2,)),
            pltpu.SemaphoreType.DMA((4,)),
        ],
        compiler_params=pltpu.CompilerParams(vmem_limit_bytes=60 * 2**20),
        name="state",
    )(keys, values)


def read_state(scale, queries, state):
    tokens = queries.shape[0]
    return pl.pallas_call(
        read_kernel,
        out_shape=jax.ShapeDtypeStruct((tokens, WIDE), jnp.bfloat16),
        in_specs=[pl.BlockSpec(memory_space=pltpu.SMEM), in_vmem(), in_vmem()],
        out_specs=in_hbm(),
        scratch_shapes=[
            pltpu.VMEM((tokens, WIDE), jnp.bfloat16),
            pltpu.VMEM((HEADS, ROWS, TILE), jnp.bfloat16),
            pltpu.VMEM((WIDE, 2 * STRIP * BAND), jnp.bfloat16),
            pltpu.SemaphoreType.DMA((tokens // TILE,)),
        ],
        compiler_params=pltpu.CompilerParams(vmem_limit_bytes=48 * 2**20),
        name="read",
    )(scale, queries, state)


def on_device(queries, keys, values):
    plane = lax.axis_size(PLANE)
    groups = lax.axis_size(("pair", "core"))
    shards = plane // groups
    layers = lax.axis_size(DEPTH)
    count = (lax.axis_index(DEPTH + ("pair", "core")) + 1).astype(jnp.float32)
    scale = (1.0 / (HD * jnp.sqrt(count * (queries.shape[0] * shards)))).reshape(1)
    order, place = 0, lax.iota(jnp.int32, layers)
    for axis in DEPTH:
        size = lax.axis_size(axis)
        order, place = order * size + place % size, place // size
    earlier = (order < lax.axis_index(DEPTH)).astype(jnp.float32)
    local = make_state(keys, values)
    part = local.shape[1:]
    local, earlier, scale = lax.optimization_barrier((local, earlier, scale))
    arrived = lax.all_to_all(local, PLANE, 0, 0, tiled=True)
    totals = jnp.sum(arrived.reshape(groups, shards, *part).astype(jnp.float32), 1)
    whole = jnp.sum(totals, 0).astype(jnp.bfloat16)
    copies = jnp.broadcast_to(whole[None], (layers, *part))
    copies, totals, earlier, scale = lax.optimization_barrier((copies, totals, earlier, scale))
    others = lax.all_to_all(copies, DEPTH[::-1], 0, 0, tiled=True)
    before = jnp.sum(others.astype(jnp.float32) * earlier[:, None, None], 0)
    running = []
    for group in range(groups):
        before = before + totals[group]
        running.append(before.astype(jnp.bfloat16))
    inclusive = jnp.stack(running)
    copies = jnp.broadcast_to(inclusive[:, None], (groups, shards, *part))
    copies, scale = lax.optimization_barrier((copies.reshape(plane, *part), scale))
    state = lax.all_to_all(copies, PLANE, 0, 0, tiled=True)
    state, scale = lax.optimization_barrier((state, scale))
    return read_state(scale, queries, state)


def solution(mesh):
    torus = Mesh(mesh.devices.reshape(2, 2, 2, 2, 2, 2, 4), EVERY)
    spec = P(EVERY, None)
    return jax.shard_map(
        on_device, mesh=torus, in_specs=(spec, spec, spec), out_specs=spec, check_vma=False
    )
```

```python
import jax
import jax.numpy as jnp
from jax import lax
from jax.experimental import pallas as pl
from jax.experimental.pallas import tpu as pltpu
from jax.sharding import Mesh
from jax.sharding import PartitionSpec as P

HD = 64
HEADS = 2
WIDE = HEADS * HD
BLOCK = 16
BLOCKS = HD // BLOCK
TURNS = BLOCK // 2
BAND = 2 * HD
ROWS = 2 * TURNS * BAND
STRIP = 9
TALL = 8
TILE = 2048
PARTS = 2 * WIDE // TALL

DEPTH = ("depth_0", "depth_1", "depth_2")
ORDER = (DEPTH[1], DEPTH[2], DEPTH[0])
PLANE = ("pair", "core", "near", "row")
EVERY = DEPTH + PLANE


def across(wide, swap, move=0, turn=0):
    rows = []
    for head in (1, 0) if swap else (0, 1):
        mine = wide[HD * head : HD * head + HD]
        if move:
            mine = jnp.concatenate([mine[BLOCK * (move % BLOCKS) :], mine[: BLOCK * (move % BLOCKS)]], 0)
        if turn:
            mine = pltpu.roll(mine, HD - turn, 0)
        rows.append(mine)
    return jnp.concatenate(rows, 0).astype(jnp.bfloat16).T


def state_kernel(keys_far, values_far, out_far, keys, values, out, arrived, left):
    loads = [
        pltpu.make_async_copy(values_far, values, arrived.at[0]),
        pltpu.make_async_copy(keys_far, keys, arrived.at[1]),
    ]
    for load in loads:
        load.start()
    stores = []

    def store(strip, begin, end):
        parts = pl.ds(WIDE // TALL * strip, WIDE // TALL)
        lanes = pl.ds(BAND * begin, BAND * (end - begin))
        stores.append(
            pltpu.make_async_copy(out.at[parts, :, lanes], out_far.at[parts, :, lanes], left.at[len(stores)])
        )
        stores[-1].start()

    def put(place, heads):
        strip, place = divmod(place, STRIP)
        for k in range(WIDE // TALL):
            head, row = divmod(k * TALL, HD)
            part = heads[head][row : row + TALL].astype(out.dtype)
            out[WIDE // TALL * strip + k, :, pl.ds(BAND * place, BAND)] = part

    loads[0].wait()
    turned_values = values[...].astype(jnp.float32).T.astype(jnp.bfloat16)
    loads[1].wait()
    x = keys[...]
    wide = x.astype(jnp.float32).T
    first = [x, across(wide, False, -1)], [across(wide, True), across(wide, True, -1)]
    lane = lax.broadcasted_iota(jnp.int32, (1, BAND), 1)

    product = jnp.dot(turned_values, x * across(wide, False, 2), preferred_element_type=jnp.float32)
    heads = [product[HD * head : HD * head + HD] for head in range(HEADS)]
    put(2 * TURNS, [jnp.where((lane < HD) == (head == 0), heads[head], 0.0) for head in range(HEADS)])
    put(2 * TURNS + 1, [jnp.zeros((HD, BAND), jnp.float32)] * HEADS)
    store(1, 2 * TURNS - STRIP, STRIP)
    for s in range(TURNS):
        others = across(wide, False, 0, s) if s else x, across(wide, True, 0, s + TURNS)
        feats = jnp.concatenate([first[swap][k] * others[swap] for k in range(2) for swap in range(2)], 1)
        product = jnp.dot(turned_values, feats, preferred_element_type=jnp.float32)
        for k in range(2):
            plain, swapped = (product[:, BAND * j : BAND * j + BAND] for j in (2 * k, 2 * k + 1))
            heads = [
                jnp.where(lane < HD, plain[:HD], swapped[:HD]),
                jnp.where(lane < HD, swapped[HD:], plain[HD:]),
            ]
            for head in range(HEADS):
                once = (lane < HD) == (head == 0) if s == 0 and k == 0 else lane < 0
                heads[head] = heads[head] * jnp.where(once, 1.0, 2.0)
            put(2 * s + k, heads)
        if 2 * s + 2 == STRIP + 1:
            store(0, 0, STRIP)
        if s == TURNS - 2:
            store(1, 0, 2 * s + 2 - STRIP)
    store(1, 2 * TURNS - 2 - STRIP, 2 * TURNS - STRIP)
    for copy in stores:
        copy.wait()


def query_band(wide, x, s):
    blocks = [x[k * BLOCK : k * BLOCK + BLOCK] for k in range(BLOCKS)]
    if s == TURNS:
        return x * jnp.concatenate(blocks[2:] + blocks[:2], 0)
    lifted = jnp.concatenate(blocks[-1:] + blocks[:-1], 0)
    others = [pltpu.roll(wide, HD - t, 0).astype(jnp.bfloat16) if t else x for t in (s, s + TURNS)]
    return [first * other for first in (x, lifted) for other in others]


def read_kernel(scale, queries, state, out_far, out, feats, whole, sent):
    for head in range(HEADS):
        for strip in range(2):
            first = WIDE // TALL * strip + HD // TALL * head
            rows = jnp.concatenate([state[first + k].astype(jnp.float32) for k in range(HD // TALL)], 0)
            whole[pl.ds(HD * head, HD), pl.ds(STRIP * BAND * strip, STRIP * BAND)] = rows.astype(jnp.bfloat16)

    def store(step):
        rows = pl.ds(pl.multiple_of(step * TILE, TILE), TILE)
        return pltpu.make_async_copy(out.at[rows], out_far.at[rows], sent.at[step])

    @pl.loop(0, out.shape[0] // TILE)
    def _(step):
        rows = pl.ds(pl.multiple_of(step * TILE, TILE), TILE)
        wide = queries[rows, :].astype(jnp.float32).T
        plain = wide.astype(jnp.bfloat16)
        heads = [pl.ds(HD * head, HD) for head in range(HEADS)]
        halves = [query_band(None, plain[HD * head : HD * head + HD], TURNS) for head in range(HEADS)]
        last = whole[:, pl.ds(2 * TURNS * BAND, BAND)]
        ends = jnp.dot(last, jnp.concatenate(halves, 0), preferred_element_type=jnp.float32)
        products = []
        for head in range(HEADS):
            here = slice(HD * head, HD * head + HD)
            for s in range(TURNS):
                parts = query_band(wide[here], plain[here], s)
                if head == 1:
                    parts = [parts[k] for k in (1, 0, 3, 2)]
                feats[head, pl.ds(2 * s * BAND, 2 * BAND), :] = jnp.concatenate(parts, 0)
            left = whole[heads[head], pl.ds(0, ROWS)]
            product = jnp.dot(left, feats[head], preferred_element_type=jnp.float32)
            products.append(ends[here] + product)
        result = jnp.concatenate(products, 0) * scale[0]
        out[rows, :] = result.T.astype(out.dtype)
        store(step).start()

    for step in range(out.shape[0] // TILE):
        store(step).wait()


def in_vmem():
    return pl.BlockSpec(memory_space=pltpu.VMEM)


def in_hbm():
    return pl.BlockSpec(memory_space=pltpu.HBM)


def make_state(keys, values):
    tokens = keys.shape[0]
    part = (TALL, STRIP * BAND)
    return pl.pallas_call(
        state_kernel,
        out_shape=jax.ShapeDtypeStruct((PARTS, *part), jnp.bfloat16),
        in_specs=[in_hbm(), in_hbm()],
        out_specs=in_hbm(),
        scratch_shapes=[
            pltpu.VMEM((tokens, WIDE), jnp.bfloat16),
            pltpu.VMEM((tokens, WIDE), jnp.bfloat16),
            pltpu.VMEM((PARTS, *part), jnp.bfloat16),
            pltpu.SemaphoreType.DMA((2,)),
            pltpu.SemaphoreType.DMA((4,)),
        ],
        compiler_params=pltpu.CompilerParams(vmem_limit_bytes=60 * 2**20),
        name="state",
    )(keys, values)


def read_state(scale, queries, state):
    tokens = queries.shape[0]
    return pl.pallas_call(
        read_kernel,
        out_shape=jax.ShapeDtypeStruct((tokens, WIDE), jnp.bfloat16),
        in_specs=[pl.BlockSpec(memory_space=pltpu.SMEM), in_vmem(), in_vmem()],
        out_specs=in_hbm(),
        scratch_shapes=[
            pltpu.VMEM((tokens, WIDE), jnp.bfloat16),
            pltpu.VMEM((HEADS, ROWS, TILE), jnp.bfloat16),
            pltpu.VMEM((WIDE, 2 * STRIP * BAND), jnp.bfloat16),
            pltpu.SemaphoreType.DMA((tokens // TILE,)),
        ],
        compiler_params=pltpu.CompilerParams(vmem_limit_bytes=48 * 2**20),
        name="read",
    )(scale, queries, state)


def on_device(queries, keys, values):
    plane = lax.axis_size(PLANE)
    groups = lax.axis_size(("pair", "core"))
    shards = plane // groups
    layers = lax.axis_size(DEPTH)
    count = (lax.axis_index(DEPTH + ("pair", "core")) + 1).astype(jnp.float32)
    scale = (1.0 / (HD * jnp.sqrt(count * (queries.shape[0] * shards)))).reshape(1)
    place = lax.iota(jnp.int32, layers)
    order = 2 * (place // 4) + 1 * (place // 2 % 2) + 4 * (place % 2)
    earlier = (order < lax.axis_index(DEPTH)).astype(jnp.float32)
    local = make_state(keys, values)
    part = local.shape[1:]
    local, earlier, scale = lax.optimization_barrier((local, earlier, scale))
    arrived = lax.all_to_all(local, PLANE, 0, 0, tiled=True)
    totals = jnp.sum(arrived.reshape(groups, shards, *part).astype(jnp.float32), 1)
    whole = jnp.sum(totals, 0).astype(jnp.bfloat16)
    copies = jnp.broadcast_to(whole[None], (layers, *part))
    copies, totals, earlier, scale = lax.optimization_barrier((copies, totals, earlier, scale))
    others = lax.all_to_all(copies, ORDER, 0, 0, tiled=True)
    before = jnp.sum(others.astype(jnp.float32) * earlier[:, None, None], 0)
    running = []
    for group in range(groups):
        before = before + totals[group]
        running.append(before.astype(jnp.bfloat16))
    inclusive = jnp.stack(running)
    copies = jnp.broadcast_to(inclusive[:, None], (groups, shards, *part))
    copies, scale = lax.optimization_barrier((copies.reshape(plane, *part), scale))
    state = lax.all_to_all(copies, PLANE, 0, 0, tiled=True)
    state, scale = lax.optimization_barrier((state, scale))
    return read_state(scale, queries, state)


def solution(mesh):
    torus = Mesh(mesh.devices.reshape(2, 2, 2, 2, 2, 2, 4), EVERY)
    spec = P(EVERY, None)
    return jax.shard_map(
        on_device, mesh=torus, in_specs=(spec, spec, spec), out_specs=spec, check_vma=False
    )
```

```python
import jax
import jax.numpy as jnp
from jax import lax
from jax.experimental import pallas as pl
from jax.experimental.pallas import tpu as pltpu
from jax.sharding import Mesh
from jax.sharding import PartitionSpec as P

HD = 64
HEADS = 2
WIDE = HEADS * HD
BLOCK = 16
BLOCKS = HD // BLOCK
TURNS = BLOCK // 2
BAND = 2 * HD
ROWS = 2 * TURNS * BAND
STRIP = 9
TALL = 8
TILE = 2048
PARTS = 2 * WIDE // TALL

DEPTH = ("depth_0", "depth_1", "depth_2")
ORDER = (DEPTH[1], DEPTH[2], DEPTH[0])
PLANE = ("pair", "core", "row", "near")
EVERY = DEPTH + ("pair", "core", "near", "row")


def across(wide, swap, move=0, turn=0):
    rows = []
    for head in (1, 0) if swap else (0, 1):
        mine = wide[HD * head : HD * head + HD]
        if move:
            mine = jnp.concatenate([mine[BLOCK * (move % BLOCKS) :], mine[: BLOCK * (move % BLOCKS)]], 0)
        if turn:
            mine = pltpu.roll(mine, HD - turn, 0)
        rows.append(mine)
    return jnp.concatenate(rows, 0).astype(jnp.bfloat16).T


def state_kernel(keys_far, values_far, out_far, keys, values, out, arrived, left):
    loads = [
        pltpu.make_async_copy(values_far, values, arrived.at[0]),
        pltpu.make_async_copy(keys_far, keys, arrived.at[1]),
    ]
    for load in loads:
        load.start()
    stores = []

    def store(strip, begin, end):
        parts = pl.ds(WIDE // TALL * strip, WIDE // TALL)
        lanes = pl.ds(BAND * begin, BAND * (end - begin))
        stores.append(
            pltpu.make_async_copy(out.at[parts, :, lanes], out_far.at[parts, :, lanes], left.at[len(stores)])
        )
        stores[-1].start()

    def put(place, heads):
        strip, place = divmod(place, STRIP)
        for k in range(WIDE // TALL):
            head, row = divmod(k * TALL, HD)
            part = heads[head][row : row + TALL].astype(out.dtype)
            out[WIDE // TALL * strip + k, :, pl.ds(BAND * place, BAND)] = part

    loads[0].wait()
    turned_values = values[...].astype(jnp.float32).T.astype(jnp.bfloat16)
    loads[1].wait()
    x = keys[...]
    wide = x.astype(jnp.float32).T
    first = [x, across(wide, False, -1)], [across(wide, True), across(wide, True, -1)]
    lane = lax.broadcasted_iota(jnp.int32, (1, BAND), 1)

    product = jnp.dot(turned_values, x * across(wide, False, 2), preferred_element_type=jnp.float32)
    heads = [product[HD * head : HD * head + HD] for head in range(HEADS)]
    put(2 * TURNS, [jnp.where((lane < HD) == (head == 0), heads[head], 0.0) for head in range(HEADS)])
    put(2 * TURNS + 1, [jnp.zeros((HD, BAND), jnp.float32)] * HEADS)
    store(1, 2 * TURNS - STRIP, STRIP)
    for s in range(TURNS):
        others = across(wide, False, 0, s) if s else x, across(wide, True, 0, s + TURNS)
        feats = jnp.concatenate([first[swap][k] * others[swap] for k in range(2) for swap in range(2)], 1)
        product = jnp.dot(turned_values, feats, preferred_element_type=jnp.float32)
        for k in range(2):
            plain, swapped = (product[:, BAND * j : BAND * j + BAND] for j in (2 * k, 2 * k + 1))
            heads = [
                jnp.where(lane < HD, plain[:HD], swapped[:HD]),
                jnp.where(lane < HD, swapped[HD:], plain[HD:]),
            ]
            for head in range(HEADS):
                once = (lane < HD) == (head == 0) if s == 0 and k == 0 else lane < 0
                heads[head] = heads[head] * jnp.where(once, 1.0, 2.0)
            put(2 * s + k, heads)
        if 2 * s + 2 == STRIP + 1:
            store(0, 0, STRIP)
        if s == TURNS - 2:
            store(1, 0, 2 * s + 2 - STRIP)
    store(1, 2 * TURNS - 2 - STRIP, 2 * TURNS - STRIP)
    for copy in stores:
        copy.wait()


def query_band(wide, x, s):
    blocks = [x[k * BLOCK : k * BLOCK + BLOCK] for k in range(BLOCKS)]
    if s == TURNS:
        return x * jnp.concatenate(blocks[2:] + blocks[:2], 0)
    lifted = jnp.concatenate(blocks[-1:] + blocks[:-1], 0)
    others = [pltpu.roll(wide, HD - t, 0).astype(jnp.bfloat16) if t else x for t in (s, s + TURNS)]
    return [first * other for first in (x, lifted) for other in others]


def read_kernel(scale, queries, state, out_far, out, feats, whole, sent):
    for head in range(HEADS):
        for strip in range(2):
            first = WIDE // TALL * strip + HD // TALL * head
            rows = jnp.concatenate([state[first + k].astype(jnp.float32) for k in range(HD // TALL)], 0)
            whole[pl.ds(HD * head, HD), pl.ds(STRIP * BAND * strip, STRIP * BAND)] = rows.astype(jnp.bfloat16)

    def store(step):
        rows = pl.ds(pl.multiple_of(step * TILE, TILE), TILE)
        return pltpu.make_async_copy(out.at[rows], out_far.at[rows], sent.at[step])

    @pl.loop(0, out.shape[0] // TILE)
    def _(step):
        rows = pl.ds(pl.multiple_of(step * TILE, TILE), TILE)
        wide = queries[rows, :].astype(jnp.float32).T
        plain = wide.astype(jnp.bfloat16)
        heads = [pl.ds(HD * head, HD) for head in range(HEADS)]
        halves = [query_band(None, plain[HD * head : HD * head + HD], TURNS) for head in range(HEADS)]
        last = whole[:, pl.ds(2 * TURNS * BAND, BAND)]
        ends = jnp.dot(last, jnp.concatenate(halves, 0), preferred_element_type=jnp.float32)
        products = []
        for head in range(HEADS):
            here = slice(HD * head, HD * head + HD)
            for s in range(TURNS):
                parts = query_band(wide[here], plain[here], s)
                if head == 1:
                    parts = [parts[k] for k in (1, 0, 3, 2)]
                feats[head, pl.ds(2 * s * BAND, 2 * BAND), :] = jnp.concatenate(parts, 0)
            left = whole[heads[head], pl.ds(0, ROWS)]
            product = jnp.dot(left, feats[head], preferred_element_type=jnp.float32)
            products.append(ends[here] + product)
        result = jnp.concatenate(products, 0) * scale[0]
        out[rows, :] = result.T.astype(out.dtype)
        store(step).start()

    for step in range(out.shape[0] // TILE):
        store(step).wait()


def in_vmem():
    return pl.BlockSpec(memory_space=pltpu.VMEM)


def in_hbm():
    return pl.BlockSpec(memory_space=pltpu.HBM)


def make_state(keys, values):
    tokens = keys.shape[0]
    part = (TALL, STRIP * BAND)
    return pl.pallas_call(
        state_kernel,
        out_shape=jax.ShapeDtypeStruct((PARTS, *part), jnp.bfloat16),
        in_specs=[in_hbm(), in_hbm()],
        out_specs=in_hbm(),
        scratch_shapes=[
            pltpu.VMEM((tokens, WIDE), jnp.bfloat16),
            pltpu.VMEM((tokens, WIDE), jnp.bfloat16),
            pltpu.VMEM((PARTS, *part), jnp.bfloat16),
            pltpu.SemaphoreType.DMA((2,)),
            pltpu.SemaphoreType.DMA((4,)),
        ],
        compiler_params=pltpu.CompilerParams(vmem_limit_bytes=60 * 2**20),
        name="state",
    )(keys, values)


def read_state(scale, queries, state):
    tokens = queries.shape[0]
    return pl.pallas_call(
        read_kernel,
        out_shape=jax.ShapeDtypeStruct((tokens, WIDE), jnp.bfloat16),
        in_specs=[pl.BlockSpec(memory_space=pltpu.SMEM), in_vmem(), in_vmem()],
        out_specs=in_hbm(),
        scratch_shapes=[
            pltpu.VMEM((tokens, WIDE), jnp.bfloat16),
            pltpu.VMEM((HEADS, ROWS, TILE), jnp.bfloat16),
            pltpu.VMEM((WIDE, 2 * STRIP * BAND), jnp.bfloat16),
            pltpu.SemaphoreType.DMA((tokens // TILE,)),
        ],
        compiler_params=pltpu.CompilerParams(vmem_limit_bytes=48 * 2**20),
        name="read",
    )(scale, queries, state)


def on_device(queries, keys, values):
    plane = lax.axis_size(PLANE)
    groups = lax.axis_size(("pair", "core"))
    shards = plane // groups
    layers = lax.axis_size(DEPTH)
    count = (lax.axis_index(DEPTH + ("pair", "core")) + 1).astype(jnp.float32)
    scale = (1.0 / (HD * jnp.sqrt(count * (queries.shape[0] * shards)))).reshape(1)
    place = lax.iota(jnp.int32, layers)
    order = 2 * (place // 4) + 1 * (place // 2 % 2) + 4 * (place % 2)
    earlier = (order < lax.axis_index(DEPTH)).astype(jnp.float32)
    local = make_state(keys, values)
    part = local.shape[1:]
    local, earlier, scale = lax.optimization_barrier((local, earlier, scale))
    arrived = lax.all_to_all(local, PLANE, 0, 0, tiled=True)
    totals = jnp.sum(arrived.reshape(groups, shards, *part).astype(jnp.float32), 1)
    whole = jnp.sum(totals, 0).astype(jnp.bfloat16)
    copies = jnp.broadcast_to(whole[None], (layers, *part))
    copies, totals, earlier, scale = lax.optimization_barrier((copies, totals, earlier, scale))
    others = lax.all_to_all(copies, ORDER, 0, 0, tiled=True)
    before = jnp.sum(others.astype(jnp.float32) * earlier[:, None, None], 0)
    running = []
    for group in range(groups):
        before = before + totals[group]
        running.append(before.astype(jnp.bfloat16))
    inclusive = jnp.stack(running)
    copies = jnp.broadcast_to(inclusive[:, None], (groups, shards, *part))
    copies, scale = lax.optimization_barrier((copies.reshape(plane, *part), scale))
    state = lax.all_to_all(copies, PLANE, 0, 0, tiled=True)
    state, scale = lax.optimization_barrier((state, scale))
    return read_state(scale, queries, state)


def solution(mesh):
    torus = Mesh(mesh.devices.reshape(2, 2, 2, 2, 2, 2, 4), EVERY)
    spec = P(EVERY, None)
    return jax.shard_map(
        on_device, mesh=torus, in_specs=(spec, spec, spec), out_specs=spec, check_vma=False
    )
```
